32 devices in a mesh: group: 4 (over y, core), dev: 8 (over z, x).
Axes of the slice: x: 2, y: 2, z: 4, core: 2. Of those that a mesh axis runs over, the one named last changes fastest.
Arguments:
- features_in: bfloat16 [96, 32768], P(None, ('group', 'dev')), may hold values from -6 to 6
- occupancy: int32 [32768], P(('group', 'dev')), may hold values 0 or 1
- cotangent: bfloat16 [96, 32768], P(None, ('group', 'dev')), may hold values from -6 to 6
- kernel_one: bfloat16 [27, 96, 96], replicated, may hold values from -0.125 to 0.125
- kernel_two: bfloat16 [27, 96, 96], replicated, may hold values from -0.125 to 0.125
- neighbours: int32 [64, 27], P(('group', 'dev')), may hold values from -1 to 5, as said below
Outputs:
- features_out: bfloat16 [96, 32768], P(None, ('group', 'dev'))
- kernel_one_grad: float32 [27, 96, 96], replicated
- kernel_two_grad: float32 [27, 96, 96], replicated
The draws below stay inside these ranges and needn't reach their ends.
Inputs may be any that keep to these rules, and one draw needn't show every extreme that they name: `neighbours`: the blocks of a device sit at distinct places of a 4 by 4 grid in y and z; the device's dev index is its slab's x position in the region. Entry 13 of a block is its own index. Other entries are -1 where no block lies at that offset (always beyond the first and last device of a region), n < 2 for block n of the same device, 2 + n for block n of the device with dev index one lower, 4 + n for block n of the device with dev index one higher; only offsets with dx = -1 or 1 reach other devices. The relation is mutual: entry t of block a names block b exactly when entry 26 - t of b names a.
All inputs are finite; a program needn't handle non-finite values. No bound on the sum of `occupancy` on one device may be relied on, other than what follows from the above.
Results may differ from the reference program's by a relative error of at most 0.0049.
Values may be sent and summed in bfloat16 or wider, within the bound.
A program may use at most 64 MiB of HBM per device.

```python
import jax
import jax.numpy as jnp
import numpy as np
from jax import lax

CH = 96
BLK = 2
PLACES = 16
GROUPS = 4
PEERS = 8
BLOCKS = 64
VOXELS = 32768


def draw_neighbours(key, part):
    keys = jax.random.split(jax.random.fold_in(key, 21), GROUPS * PEERS)
    perms = jax.vmap(lambda one_key: jax.random.permutation(one_key, PLACES))(keys)
    spots = perms.reshape(GROUPS, PEERS, PLACES)[:, :, :BLK].astype(jnp.int32)
    place_ids = jnp.arange(PLACES, dtype=jnp.int32)
    block_ids = jnp.arange(BLK, dtype=jnp.int32)
    hits = spots[:, :, :, None] == place_ids[None, None, None, :]
    owned = jnp.sum(jnp.where(hits, block_ids[None, None, :, None], 0), axis=2)
    index_at = jnp.where(jnp.any(hits, axis=2), owned, -1).astype(jnp.int32)
    empty_row = jnp.full((GROUPS, 1, PLACES), -1, jnp.int32)
    index_pad = jnp.concatenate([empty_row, index_at, empty_row], axis=1)
    coord_y = spots // 4
    coord_z = spots % 4
    entries = []
    for step_x in (-1, 0, 1):
        rows = index_pad[:, 1 + step_x:1 + step_x + PEERS, :]
        base = 0 if step_x == 0 else BLK if step_x < 0 else 2 * BLK
        for step_y in (-1, 0, 1):
            for step_z in (-1, 0, 1):
                target_y = coord_y + step_y
                target_z = coord_z + step_z
                inside = (target_y >= 0) & (target_y < 4) & (target_z >= 0) & (target_z < 4)
                place = jnp.clip(target_y, 0, 3) * 4 + jnp.clip(target_z, 0, 3)
                found = jnp.take_along_axis(rows, place, axis=2)
                entries.append(jnp.where(inside & (found >= 0), found + base, -1))
    stacked = jnp.stack(entries, axis=-1)
    return stacked.reshape(BLOCKS, 27).astype(jnp.int32)


def place_ends(values, rng, smallest, top_value):
    shape = values.shape
    spot = [jax.random.randint(jax.random.fold_in(rng, axis), (), 0, shape[axis]) for axis in range(len(shape))]
    values = values.at[tuple(spot)].set(smallest)
    longest = shape.index(max(shape))
    spot[longest] = (spot[longest] + 1) % shape[longest]
    return values.at[tuple(spot)].set(top_value)


def level_of(own_key, shape, cuts, smallest, high):
    level = 1.0
    for dim, shards_of in cuts:
        heights = jax.random.uniform(jax.random.fold_in(jax.random.fold_in(own_key, 6), dim), (shards_of,), jnp.float32, smallest / len(cuts), high / len(cuts))
        level = level * jnp.repeat(jnp.exp(heights), shape[dim] // shards_of).reshape((-1,) + (1,) * (len(shape) - 1 - dim))
    return level


def noise(rng, dims, scale, reach, cuts=(), kind=jnp.bfloat16):
    drawn = scale * jax.random.normal(rng, dims, jnp.float32)
    if cuts:
        drawn = drawn * level_of(rng, dims, cuts, -0.22, 0.18)
    return jnp.clip(drawn, -reach, reach).astype(kind)


def setup_inputs(seed: int = 0) -> dict:
    key_list = jax.random.split(jax.random.key(seed), 7)
    features_in = noise(key_list[0], (CH, VOXELS), 1.0, 6.0, ((1, 32),))
    occupancy = place_ends((jax.random.randint(key_list[1], (VOXELS,), 0, 5) < 3).astype(jnp.int32), jax.random.fold_in(key_list[1], 1), 0, 1)
    cotangent = noise(key_list[2], (CH, VOXELS), 1.0, 6.0, ((1, 32),))
    kernel_one = noise(key_list[3], (27, CH, CH), (27 * CH) ** -0.5, 0.125)
    kernel_two = noise(key_list[4], (27, CH, CH), (27 * CH) ** -0.5, 0.125)
    neighbours = draw_neighbours(jax.random.fold_in(key_list[6], 71), 0)
    return dict(features_in=features_in, occupancy=occupancy, cotangent=cotangent, kernel_one=kernel_one, kernel_two=kernel_two, neighbours=neighbours)


def pad_tables():
    cells = np.arange(1000)
    coord_x = cells // 100
    coord_y = cells // 10 % 10
    coord_z = cells % 10

    def side(coord):
        return np.where(coord == 0, -1, np.where(coord == 9, 1, 0))

    def inner(coord):
        return np.where(coord == 0, 7, np.where(coord == 9, 0, coord - 1))
    offset_of = (side(coord_x) + 1) * 9 + (side(coord_y) + 1) * 3 + (side(coord_z) + 1)
    voxel_of = inner(coord_x) * 64 + inner(coord_y) * 8 + inner(coord_z)
    return (offset_of.astype(np.int32), voxel_of.astype(np.int32))

def cube_window(cube, first, second, third, width):
    return cube[:, :, first:first + 8, second:second + 8, third:third + 8].reshape(width, -1)

def conv_forward(padded, kernel):
    width = padded.shape[0]
    cube = padded.reshape(width, -1, 10, 10, 10)
    total = None
    for first in range(3):
        for second in range(3):
            stacked = jnp.concatenate([cube_window(cube, first, second, third, width) for third in range(3)], axis=0)
            start = first * 9 + second * 3
            weights = kernel[start:start + 3].reshape(3 * width, width)
            term = lax.dot_general(weights, stacked, (((0,), (0,)), ((), ())), preferred_element_type=jnp.float32)
            total = term if total is None else total + term
    return total

def kernel_terms(padded, grad):
    width = padded.shape[0]
    cube = padded.reshape(width, -1, 10, 10, 10)
    pieces = []
    for first in range(3):
        for second in range(3):
            stacked = jnp.concatenate([cube_window(cube, first, second, third, width) for third in range(3)], axis=0)
            term = lax.dot_general(stacked, grad, (((1,), (1,)), ((), ())), preferred_element_type=jnp.float32)
            pieces.append(term.reshape(3, width, width))
    return jnp.concatenate(pieces, axis=0)

def conv_backward(padded, kernel):
    width = padded.shape[0]
    cube = padded.reshape(width, -1, 10, 10, 10)
    total = None
    for first in range(3):
        for second in range(3):
            stacked = jnp.concatenate([cube_window(cube, 2 - first, 2 - second, 2 - third, width) for third in range(3)], axis=0)
            start = first * 9 + second * 3
            weights = jnp.concatenate([kernel[start + third] for third in range(3)], axis=1)
            term = jnp.dot(weights, stacked, preferred_element_type=jnp.float32)
            total = term if total is None else total + term
    return total

def global_neighbours(neighbours):
    owner = (jnp.arange(BLOCKS, dtype=jnp.int32) // BLK)[:, None]
    here = owner * BLK + neighbours
    lower = (owner - 1) * BLK + neighbours - BLK
    upper = (owner + 1) * BLK + neighbours - 2 * BLK
    found = jnp.where(neighbours < BLK, here, jnp.where(neighbours < 2 * BLK, lower, upper))
    return jnp.where(neighbours < 0, BLOCKS, found).astype(jnp.int32)

def reference(features_in, occupancy, cotangent, kernel_one, kernel_two, neighbours):
    offset_np, voxel_np = pad_tables()
    offset_of = jnp.asarray(offset_np)
    voxel_of = jnp.asarray(voxel_np)
    devices = BLOCKS // BLK
    span = BLK * 512
    where_nb = global_neighbours(neighbours)
    mask = occupancy.astype(jnp.float32)[None, :]
    occupied = occupancy[None, :] > 0
    scale = float(VOXELS) ** (-0.5)
    device_ids = jnp.arange(devices, dtype=jnp.int32)

    def with_zero(values):
        return jnp.concatenate([values, jnp.zeros((CH, 512), values.dtype)], axis=1)

    def padded_at(table, device):
        rows = lax.dynamic_slice_in_dim(where_nb, device * BLK, BLK, 0)
        columns = rows[:, offset_of] * 512 + voxel_of[None, :]
        return jnp.take(table, columns.reshape(-1), axis=1)

    def spread(stacked):
        return jnp.transpose(stacked, (1, 0, 2)).reshape(CH, VOXELS)

    def forward(values, kernel):
        table = with_zero(values)
        return spread(lax.map(lambda device: conv_forward(padded_at(table, device), kernel), device_ids))

    def backward(values, kernel):
        table = with_zero(values)
        return spread(lax.map(lambda device: conv_backward(padded_at(table, device), kernel), device_ids))

    def kernel_grad(values, grad):
        table = with_zero(values)

        def one(device):
            piece = lax.dynamic_slice_in_dim(grad, device * span, span, 1)
            return kernel_terms(padded_at(table, device), piece)
        return scale * lax.optimization_barrier(jnp.sum(lax.map(one, device_ids), axis=0))
    a_zero = jnp.where(occupied, features_in, jnp.zeros_like(features_in))
    z_one = mask * forward(a_zero, kernel_one)
    a_one = jax.nn.silu(z_one).astype(jnp.bfloat16)
    features_out = (mask * forward(a_one, kernel_two)).astype(jnp.bfloat16)
    g_two = jnp.where(occupied, cotangent, jnp.zeros_like(cotangent))
    kernel_two_grad = kernel_grad(a_one, g_two)
    ga_one = mask * backward(g_two, kernel_two)
    sigma = jax.nn.sigmoid(z_one)
    gz_one = (ga_one * sigma * (1.0 + z_one * (1.0 - sigma))).astype(jnp.bfloat16)
    kernel_one_grad = kernel_grad(a_zero, gz_one)
    return (features_out, kernel_one_grad, kernel_two_grad)
```

```python
import functools
import math

import jax
import jax.numpy as jnp
from jax import lax
from jax.experimental import pallas as pl
from jax.experimental.pallas import tpu as pltpu
from jax.sharding import PartitionSpec as P

LANES = 128
TAPS = 27
PLANE = 64
F32 = jnp.float32
BF16 = jnp.bfloat16


def build_windows(blocks, local, lower, upper, near, q, cols):
    row = lax.broadcasted_iota(jnp.int32, (1, 8, LANES), 1)

    def shifted(main, before, after):
        down = jnp.where(row == 0, pltpu.roll(before, 1, 1), pltpu.roll(main, 1, 1))
        up = jnp.where(row == 7, pltpu.roll(after, 7, 1), pltpu.roll(main, 7, 1))
        return down, main, up

    for b in range(blocks):
        for tx in range(3):
            for ty in range(3):
                src_y = (slice(7, 8), slice(0, 8), slice(0, 1))[ty]
                dst_y = (slice(0, 1), slice(1, 9), slice(9, 10))[ty]
                dst_x = (slice(0, 1), slice(1, 9), slice(9, 10))[tx]
                rows_y = src_y.stop - src_y.start
                rows_x = dst_x.stop - dst_x.start
                parts = []
                for tz in range(3):
                    n = near[b, tx * 9 + ty * 3 + tz]
                    if tx == 1:
                        index = jnp.where(n < 0, blocks, n)
                        value = local[index, :, src_y]
                    elif tx == 0:
                        index = jnp.where(n < 0, blocks, n - blocks)
                        value = lower[index, src_y]
                    else:
                        index = jnp.where(n < 0, blocks, n - 2 * blocks)
                        value = upper[index, src_y]
                    parts.append(value.reshape(rows_x * rows_y, 8, LANES))
                moved = shifted(parts[1], parts[0], parts[2])
                for dz in range(3):
                    q[dz, b, dst_x, dst_y] = moved[dz].reshape(rows_x, rows_y, 8, LANES)
        for dy in range(3):
            for dz in range(3):
                k = dy * 3 + dz
                window = q[dz, b, :, dy : dy + 8].reshape(10 * PLANE, LANES)
                cols[b, :, k * LANES : (k + 1) * LANES] = window.astype(BF16)


def tall(values, width):
    values = values.astype(F32)
    filler = jnp.zeros((LANES - width, values.shape[1]), F32)
    return jnp.concatenate([values, filler], axis=0).T


def first_kernel(
    blocks, width, feat, cot, occ, low_in, high_in, one, two, near,
    a_out, rim_first, rim_last, terms,
    local, rims, q, cols_a, cols_g, weight_one, weight_two, spread,
):
    taps = 9 * LANES
    span = 8 * PLANE
    mask_row = (occ[...] > 0).astype(F32)
    mask = jnp.broadcast_to(mask_row, (LANES, blocks * span)).T
    for kind, source in ((0, feat), (1, cot)):
        value = tall(source[...].astype(F32) * mask_row, width)
        local[kind, 0:blocks] = value.reshape(blocks, 8, 8, 8, LANES)
        local[kind, blocks] = jnp.zeros((8, 8, 8, LANES), F32)
        for side, arrived in ((0, low_in), (1, high_in)):
            rim = tall(arrived[kind * width : (kind + 1) * width, :], width)
            rims[kind, side, 0:blocks] = rim.reshape(blocks, 8, 8, LANES)
            rims[kind, side, blocks] = jnp.zeros((8, 8, LANES), F32)
    weight_one[...] = jnp.zeros_like(weight_one)
    weight_two[...] = jnp.zeros_like(weight_two)
    for t in range(TAPS):
        weight_one[t * LANES : t * LANES + width, 0:width] = one[t]
        weight_two[0:width, t * LANES : t * LANES + width] = two[TAPS - 1 - t]
    spread[...] = jnp.zeros_like(spread)

    build_windows(blocks, local.at[0], rims.at[0, 0], rims.at[0, 1], near, q, cols_a)
    build_windows(blocks, local.at[1], rims.at[1, 0], rims.at[1, 1], near, q, cols_g)
    for b in range(blocks):
        z = jnp.zeros((span, LANES), F32)
        ga = jnp.zeros((span, LANES), F32)
        for dx in range(3):
            rows = slice(dx * PLANE, dx * PLANE + span)
            z += jnp.dot(
                cols_a[b, rows, :],
                weight_one[dx * taps : (dx + 1) * taps, :],
                preferred_element_type=F32,
            )
            ga += lax.dot_general(
                cols_g[b, rows, :],
                weight_two[:, dx * taps : (dx + 1) * taps],
                (((1,), (1,)), ((), ())),
                preferred_element_type=F32,
            )
        inside = mask[b * span : (b + 1) * span]
        z = z * inside
        ga = ga * inside
        sigma = 1.0 / (1.0 + jnp.exp(-z))
        hidden = (z * sigma).astype(BF16)
        gz = (ga * sigma * (1.0 + z * (1.0 - sigma))).astype(BF16)
        a_out[b * span : (b + 1) * span, :] = hidden
        rim_first[b * PLANE : (b + 1) * PLANE, :] = hidden[0:PLANE]
        rim_last[b * PLANE : (b + 1) * PLANE, :] = hidden[span - PLANE : span]
        for dx in range(3):
            rows = slice(dx * PLANE, dx * PLANE + span)
            spread[0, b, rows, dx * LANES : (dx + 1) * LANES] = gz
            spread[1, b, rows, dx * LANES : (dx + 1) * LANES] = hidden
    sums = []
    for kind, cols in ((0, cols_a), (1, cols_g)):
        total = None
        for b in range(blocks):
            part = lax.dot_general(
                spread[kind, b], cols[b], (((0,), (0,)), ((), ())), preferred_element_type=F32
            )
            total = part if total is None else total + part
        sums.append(total)

    def matrix(j):
        if j < TAPS:
            dx, k = j // 9, j % 9
            block = sums[0][dx * LANES : (dx + 1) * LANES, k * LANES : (k + 1) * LANES]
            return block.T[0:width]
        t = 2 * TAPS - 1 - j
        dx, k = t // 9, t % 9
        return sums[1][dx * LANES : dx * LANES + width, k * LANES : (k + 1) * LANES]

    main, folded = fold_counts(width)
    lane = lax.broadcasted_iota(jnp.int32, (width, LANES), 1)
    room = LANES - width
    each = width // room
    for j in range(main):
        value = matrix(j)
        if j // each < folded:
            extra = matrix(main + j // each)
            chunk = j % each
            extra = pltpu.roll(extra, (width - room * chunk) % LANES, 1)
            value = jnp.where(lane < width, value, extra)
        terms[j * width : (j + 1) * width, :] = value.astype(BF16)
    for j in range(main + folded, 2 * TAPS):
        place = j - folded
        terms[place * width : (place + 1) * width, :] = matrix(j).astype(BF16)
    used = (2 * TAPS - folded) * width
    terms[used:, :] = jnp.zeros((terms.shape[0] - used, LANES), BF16)


def fold_counts(width):
    each = width // (LANES - width)
    folded = 2 * TAPS // (each + 1)
    return folded * each, folded


def sum_kernel(orders, sizes, terms, total, work, landing, whole, send_sem, recv_sem):
    place = {axis: lax.axis_index(axis) for axis in sizes}
    partners = {}
    for axis, bit in orders[0]:
        mine = (place[axis] // (1 << bit)) % 2
        partners[axis, bit] = (mine, place[axis] + (1 - 2 * mine) * (1 << bit))
    barrier = pltpu.get_barrier_semaphore()
    for (axis, _), (_, other) in partners.items():
        pl.semaphore_signal(
            barrier, inc=1, device_id={axis: other}, device_id_type=pl.DeviceIdType.MESH
        )
    pl.semaphore_wait(barrier, len(partners))

    steps = len(orders[0])
    rows = terms.shape[0] // len(orders)
    bases = [s * rows for s in range(len(orders))]
    at = [s * rows for s in range(len(orders))]
    length = rows

    def ds(start, size):
        return pl.ds(pl.multiple_of(start, 16), size)

    for step in range(steps):
        half = length // 2
        source = terms if step == 0 else work
        target = whole if step == steps - 1 else work
        copies = []
        for s, order in enumerate(orders):
            axis, bit = order[step]
            mine, other = partners[axis, bit]
            copy = pltpu.make_async_remote_copy(
                src_ref=source.at[ds(bases[s] + (1 - mine) * half, half)],
                dst_ref=landing.at[pl.ds(at[s], half)],
                send_sem=send_sem.at[s, step],
                recv_sem=recv_sem.at[s, step],
                device_id={axis: other},
                device_id_type=pl.DeviceIdType.MESH,
            )
            copy.start()
            copies.append(copy)
        for s, order in enumerate(orders):
            mine, _ = partners[order[step]]
            copies[s].wait()
            keep = bases[s] + mine * half
            value = source[ds(keep, half), :].astype(F32)
            value += landing[at[s] : at[s] + half, :].astype(F32)
            target[ds(keep, half), :] = value.astype(BF16)
            bases[s] = keep
            at[s] += half
        length = half
    for step in reversed(range(steps)):
        copies = []
        for s, order in enumerate(orders):
            axis, bit = order[step]
            _, other = partners[axis, bit]
            here = whole.at[ds(bases[s], length)]
            copy = pltpu.make_async_remote_copy(
                src_ref=here,
                dst_ref=here,
                send_sem=send_sem.at[s, steps + step],
                recv_sem=recv_sem.at[s, steps + step],
                device_id={axis: other},
                device_id_type=pl.DeviceIdType.MESH,
            )
            copy.start()
            copies.append(copy)
        for s, order in enumerate(orders):
            copies[s].wait()
            mine, _ = partners[order[step]]
            bases[s] = bases[s] - mine * length
        length *= 2
    total[...] = whole[...]


def last_kernel(
    blocks, width, scale, hidden, low_in, high_in, occ, two, near, total,
    out, grad_one, grad_two, local, rims, q, cols, weight,
):
    taps = 9 * LANES
    span = 8 * PLANE
    local[0:blocks] = hidden[...].astype(F32).reshape(blocks, 8, 8, 8, LANES)
    local[blocks] = jnp.zeros((8, 8, 8, LANES), F32)
    for side, arrived in ((0, low_in), (1, high_in)):
        rims[side, 0:blocks] = arrived[...].astype(F32).reshape(blocks, 8, 8, LANES)
        rims[side, blocks] = jnp.zeros((8, 8, LANES), F32)
    weight[...] = jnp.zeros_like(weight)
    for t in range(TAPS):
        weight[t * LANES : t * LANES + width, 0:width] = two[t]
    build_windows(blocks, local, rims.at[0], rims.at[1], near, q, cols)
    mask_row = (occ[...] > 0).astype(F32)
    for b in range(blocks):
        y = jnp.zeros((span, LANES), F32)
        for dx in range(3):
            y += jnp.dot(
                cols[b, dx * PLANE : dx * PLANE + span, :],
                weight[dx * taps : (dx + 1) * taps, :],
                preferred_element_type=F32,
            )
        here = slice(b * span, (b + 1) * span)
        out[:, here] = (y.T[0:width] * mask_row[:, here]).astype(BF16)

    main, folded = fold_counts(width)
    each = main // folded

    def rows(place):
        return total[place * width : (place + 1) * width, :].astype(F32) * scale

    def put(j, value):
        if j < TAPS:
            grad_one[j] = value
        else:
            grad_two[j - TAPS] = value

    for group in range(folded):
        spare = []
        for chunk in range(each):
            value = rows(group * each + chunk)
            put(group * each + chunk, value[:, 0:width])
            spare.append(value[:, width:LANES])
        put(main + group, jnp.concatenate(spare, axis=1))
    for j in range(main + folded, 2 * TAPS):
        put(j, rows(j - folded)[:, 0:width])


def bits_of(axis, size):
    return [(axis, bit) for bit in range(size.bit_length() - 1)]


def per_device(sizes, features_in, occupancy, cotangent, kernel_one, kernel_two, neighbours):
    width, span = features_in.shape
    blocks = neighbours.shape[0]
    devices = math.prod(sizes.values())
    scale = float(span * devices) ** (-0.5)
    vmem = pl.BlockSpec(memory_space=pltpu.VMEM)
    smem = pl.BlockSpec(memory_space=pltpu.SMEM)
    params = pltpu.CompilerParams(vmem_limit_bytes=48 * 1024 * 1024)
    occ = occupancy[None, :]
    count = sizes["dev"]
    forward = [(i, i + 1) for i in range(count - 1)]
    backward = [(target, source) for source, target in forward]

    def plane(values, x):
        return values.reshape(width, blocks, 8, PLANE)[:, :, x].reshape(width, -1)

    def rim(x):
        both = jnp.concatenate([plane(features_in, x), plane(cotangent, x)], axis=0)
        inside = occupancy.reshape(blocks, 8, PLANE)[:, x].reshape(1, -1) > 0
        return jnp.where(inside, both, jnp.zeros_like(both))

    low = lax.ppermute(rim(7), "dev", forward)
    high = lax.ppermute(rim(0), "dev", backward)

    orders = [
        bits_of("group", sizes["group"])[:1]
        + bits_of("dev", sizes["dev"])[:1]
        + bits_of("group", sizes["group"])[1:]
        + bits_of("dev", sizes["dev"])[1:],
        bits_of("group", sizes["group"]) + bits_of("dev", sizes["dev"]),
    ]
    steps = len(orders[0])
    streams = len(orders)
    _, folded = fold_counts(width)
    used = (2 * TAPS - folded) * width
    unit = 16 * devices * streams
    rows = -(-used // unit) * unit

    hidden, rim_first, rim_last, terms = pl.pallas_call(
        functools.partial(first_kernel, blocks, width),
        out_shape=(
            jax.ShapeDtypeStruct((span, LANES), BF16),
            jax.ShapeDtypeStruct((blocks * PLANE, LANES), BF16),
            jax.ShapeDtypeStruct((blocks * PLANE, LANES), BF16),
            jax.ShapeDtypeStruct((rows, LANES), BF16),
        ),
        in_specs=[vmem] * 7 + [smem],
        out_specs=[vmem] * 4,
        scratch_shapes=[
            pltpu.VMEM((2, blocks + 1, 8, 8, 8, LANES), F32),
            pltpu.VMEM((2, 2, blocks + 1, 8, 8, LANES), F32),
            pltpu.VMEM((3, blocks, 10, 10, 8, LANES), F32),
            pltpu.VMEM((blocks, 10 * PLANE, 9 * LANES), BF16),
            pltpu.VMEM((blocks, 10 * PLANE, 9 * LANES), BF16),
            pltpu.VMEM((TAPS * LANES, LANES), BF16),
            pltpu.VMEM((LANES, TAPS * LANES), BF16),
            pltpu.VMEM((2, blocks, 10 * PLANE, 3 * LANES), BF16),
        ],
        compiler_params=params,
        name="first_layer",
    )(features_in, cotangent, occ, low, high, kernel_one, kernel_two, neighbours)

    low = lax.ppermute(rim_last, "dev", forward)
    high = lax.ppermute(rim_first, "dev", backward)

    total = pl.pallas_call(
        functools.partial(sum_kernel, orders, sizes),
        out_shape=jax.ShapeDtypeStruct((rows, LANES), BF16),
        in_specs=[vmem],
        out_specs=vmem,
        scratch_shapes=[
            pltpu.VMEM((rows, LANES), BF16),
            pltpu.VMEM((rows, LANES), BF16),
            pltpu.VMEM((rows, LANES), BF16),
            pltpu.SemaphoreType.DMA((streams, 2 * steps)),
            pltpu.SemaphoreType.DMA((streams, 2 * steps)),
        ],
        compiler_params=pltpu.CompilerParams(
            collective_id=0, has_side_effects=True, vmem_limit_bytes=48 * 1024 * 1024
        ),
        name="sum_terms",
    )(terms)

    return pl.pallas_call(
        functools.partial(last_kernel, blocks, width, scale),
        out_shape=(
            jax.ShapeDtypeStruct((width, span), BF16),
            jax.ShapeDtypeStruct((TAPS, width, width), F32),
            jax.ShapeDtypeStruct((TAPS, width, width), F32),
        ),
        in_specs=[vmem] * 5 + [smem, vmem],
        out_specs=[vmem] * 3,
        scratch_shapes=[
            pltpu.VMEM((blocks + 1, 8, 8, 8, LANES), F32),
            pltpu.VMEM((2, blocks + 1, 8, 8, LANES), F32),
            pltpu.VMEM((3, blocks, 10, 10, 8, LANES), F32),
            pltpu.VMEM((blocks, 10 * PLANE, 9 * LANES), BF16),
            pltpu.VMEM((TAPS * LANES, LANES), BF16),
        ],
        compiler_params=params,
        name="second_layer",
    )(hidden, low, high, occ, kernel_two, neighbours, total)


def solution(mesh):
    sizes = dict(mesh.shape)
    return jax.shard_map(
        functools.partial(per_device, sizes),
        mesh=mesh,
        in_specs=(
            P(None, ("group", "dev")),
            P(("group", "dev")),
            P(None, ("group", "dev")),
            P(),
            P(),
            P(("group", "dev"), None),
        ),
        out_specs=(P(None, ("group", "dev")), P(), P()),
        check_vma=False,
    )
```

```python
import functools
import math

import jax
import jax.numpy as jnp
from jax import lax
from jax.experimental import pallas as pl
from jax.experimental.pallas import tpu as pltpu
from jax.sharding import PartitionSpec as P

LANES = 128
TAPS = 27
PLANE = 64
F32 = jnp.float32
BF16 = jnp.bfloat16


def build_windows(blocks, local, lower, upper, near, q, cols):
    row = lax.broadcasted_iota(jnp.int32, (1, 8, LANES), 1)

    def shifted(main, before, after):
        down = jnp.where(row == 0, pltpu.roll(before, 1, 1), pltpu.roll(main, 1, 1))
        up = jnp.where(row == 7, pltpu.roll(after, 7, 1), pltpu.roll(main, 7, 1))
        return down, main, up

    for b in range(blocks):
        for tx in range(3):
            for ty in range(3):
                src_y = (slice(7, 8), slice(0, 8), slice(0, 1))[ty]
                dst_y = (slice(0, 1), slice(1, 9), slice(9, 10))[ty]
                dst_x = (slice(0, 1), slice(1, 9), slice(9, 10))[tx]
                rows_y = src_y.stop - src_y.start
                rows_x = dst_x.stop - dst_x.start
                parts = []
                for tz in range(3):
                    n = near[b, tx * 9 + ty * 3 + tz]
                    n = n - (blocks, 0, 2 * blocks)[tx]
                    index = jnp.where((n >= 0) & (n < blocks), n, blocks)
                    if tx == 1:
                        value = local[index, :, src_y]
                    else:
                        value = (lower, None, upper)[tx][index, src_y]
                    parts.append(value.reshape(rows_x * rows_y, 8, LANES))
                moved = shifted(parts[1], parts[0], parts[2])
                for dz in range(3):
                    q[dz, b, dst_x, dst_y] = moved[dz].reshape(rows_x, rows_y, 8, LANES)
        for dy in range(3):
            for dz in range(3):
                k = dy * 3 + dz
                window = q[dz, b, :, dy : dy + 8].reshape(10 * PLANE, LANES)
                cols[b, :, k * LANES : (k + 1) * LANES] = window.astype(BF16)


def tall(values, width):
    values = values.astype(F32)
    filler = jnp.zeros((LANES - width, values.shape[1]), F32)
    return jnp.concatenate([values, filler], axis=0).T


def fold_counts(width):
    each = width // (LANES - width)
    folded = TAPS // (each + 1)
    return folded * each, folded


def fold(terms, start, rows, width, matrix):
    main, folded = fold_counts(width)
    lane = lax.broadcasted_iota(jnp.int32, (width, LANES), 1)
    room = LANES - width
    each = width // room
    for j in range(main):
        chunk = j % each
        extra = pltpu.roll(matrix(main + j // each), (width - room * chunk) % LANES, 1)
        at = start + j * width
        terms[at : at + width, :] = jnp.where(lane < width, matrix(j), extra)
    for j in range(main + folded, TAPS):
        at = start + (j - folded) * width
        terms[at : at + width, :] = matrix(j)
    used = (TAPS - folded) * width
    terms[start + used : start + rows, :] = jnp.zeros((rows - used, LANES), F32)


class Stream:
    def __init__(self, number, start, rows, order, place, refs):
        self.number, self.base, self.length, self.order = number, start, rows, order
        self.at = start
        self.place = place
        self.terms, self.stage, self.landing, self.whole, self.send_sem, self.recv_sem = refs
        self.step = 0
        self.copies = []
        self.sent = []
        self.slot = 0

    def ds(self, start, size):
        return pl.ds(pl.multiple_of(start, 16), size)

    def send(self, src, dst, axis, other):
        copy = pltpu.make_async_remote_copy(
            src_ref=src,
            dst_ref=dst,
            send_sem=self.send_sem.at[self.number, self.slot],
            recv_sem=self.recv_sem.at[self.number, self.slot],
            device_id={axis: other},
            device_id_type=pl.DeviceIdType.MESH,
        )
        copy.start()
        self.slot += 1
        self.copies.append(copy)
        self.sent.append(copy)

    def start(self):
        count = len(self.order)
        self.copies = []
        if self.step < count:
            axis, low, radix = self.order[self.step]
            digit, others = peers(self.place, axis, low, radix)
            chunk = self.length // radix
            self.slots = []
            for theirs, other in others:
                here = slice(self.at, self.at + chunk)
                values = self.terms[self.ds(self.base + theirs * chunk, chunk), :]
                self.stage[here, :] = values.astype(BF16)
                rows = pl.ds(self.at, chunk)
                self.send(self.stage.at[rows], self.landing.at[rows], axis, other)
                self.slots.append(here)
                self.at += chunk
        else:
            axis, low, radix = self.order[2 * count - 1 - self.step]
            _, others = peers(self.place, axis, low, radix)
            here = self.whole.at[self.ds(self.base, self.length)]
            for _, other in others:
                self.send(here, here, axis, other)

    def finish(self):
        count = len(self.order)
        for copy in self.copies:
            copy.wait_recv()
        if self.step < count:
            axis, low, radix = self.order[self.step]
            digit, _ = peers(self.place, axis, low, radix)
            chunk = self.length // radix
            keep = self.base + digit * chunk
            value = self.terms[self.ds(keep, chunk), :]
            for here in self.slots:
                value = value + self.landing[here, :].astype(F32)
            if self.step == count - 1:
                self.whole[self.ds(keep, chunk), :] = value.astype(BF16)
            else:
                self.terms[self.ds(keep, chunk), :] = value
            self.base, self.length = keep, chunk
        else:
            axis, low, radix = self.order[2 * count - 1 - self.step]
            digit, _ = peers(self.place, axis, low, radix)
            self.base = self.base - digit * self.length
            self.length *= radix
        self.step += 1

    def done(self):
        return self.step == 2 * len(self.order)

    def advance(self):
        if not self.done():
            self.finish()
            if not self.done():
                self.start()

    def close(self):
        for copy in self.sent:
            copy.wait_send()


def peers(place, axis, low, radix):
    unit = 1 << low
    digit = (place[axis] // unit) % radix
    others = []
    for step in range(1, radix):
        theirs = (digit + step) % radix
        others.append((theirs, place[axis] + (theirs - digit) * unit))
    return digit, others


def step_kernel(
    blocks, width, sizes, orders, stream_rows,
    feat, cot, occ, one, two, near,
    out, total,
    local_a, local_g, low_a, high_a, low_g, high_g, q, cols_a, cols_g, weight_one, weight_two,
    spread_a, spread_g, send_first, send_last, land_low, land_high,
    hidden_first, hidden_last, hidden_low, hidden_high,
    terms, stage, landing, whole, send_sem, recv_sem, rim_send, rim_recv,
):
    taps = 9 * LANES
    span = 8 * PLANE
    rim_rows = blocks * PLANE
    place = {axis: lax.axis_index(axis) for axis in sizes}
    dev, count = place["dev"], sizes["dev"]
    has_low = dev > 0
    has_high = dev < count - 1
    low_dev = (dev + count - 1) % count
    high_dev = (dev + 1) % count

    for ref in (land_low, land_high, hidden_low, hidden_high):
        ref[...] = jnp.zeros_like(ref)

    barrier = pltpu.get_barrier_semaphore()

    def greet(axis, other):
        pl.semaphore_signal(
            barrier, inc=1, device_id={axis: other}, device_id_type=pl.DeviceIdType.MESH
        )

    greeted = 0
    for phase in orders[0]:
        for _, other in peers(place, *phase)[1]:
            greet(phase[0], other)
            greeted += 1

    @pl.when(has_low)
    def _():
        greet("dev", low_dev)

    @pl.when(has_high)
    def _():
        greet("dev", high_dev)

    def rim_copy(which, src, dst, other):
        return pltpu.make_async_remote_copy(
            src_ref=src,
            dst_ref=dst,
            send_sem=rim_send.at[which],
            recv_sem=rim_recv.at[which],
            device_id={"dev": other},
            device_id_type=pl.DeviceIdType.MESH,
        )

    rim_copies = [
        rim_copy(0, send_last, land_low, high_dev),
        rim_copy(1, send_first, land_high, low_dev),
        rim_copy(2, hidden_last, hidden_low, high_dev),
        rim_copy(3, hidden_first, hidden_high, low_dev),
    ]

    def rims_go(first):
        @pl.when(has_high)
        def _():
            rim_copies[first].start()

        @pl.when(has_low)
        def _():
            rim_copies[first + 1].start()

    def rims_here(first):
        @pl.when(has_low)
        def _():
            rim_copies[first].wait_recv()

        @pl.when(has_high)
        def _():
            rim_copies[first + 1].wait_recv()

    def rims_gone(first):
        @pl.when(has_high)
        def _():
            rim_copies[first].wait_send()

        @pl.when(has_low)
        def _():
            rim_copies[first + 1].wait_send()

    mask_row = (occ[...] > 0).astype(F32)
    for kind, source, local in ((0, feat, local_a), (1, cot, local_g)):
        value = tall(source[...].astype(F32) * mask_row, width)
        local[0:blocks] = value.reshape(blocks, 8, 8, 8, LANES)
        local[blocks] = jnp.zeros((8, 8, 8, LANES), F32)
        for b in range(blocks):
            at = kind * rim_rows + b * PLANE
            send_first[at : at + PLANE, :] = value[b * span : b * span + PLANE].astype(BF16)
            send_last[at : at + PLANE, :] = value[(b + 1) * span - PLANE : (b + 1) * span].astype(BF16)

    pl.semaphore_wait(barrier, greeted + has_low.astype(jnp.int32) + has_high.astype(jnp.int32))
    rims_go(0)

    mask = jnp.broadcast_to(mask_row, (LANES, blocks * span)).T
    weight_one[...] = jnp.zeros_like(weight_one)
    weight_two[...] = jnp.zeros_like(weight_two)
    for t in range(TAPS):
        weight_one[t * LANES : t * LANES + width, 0:width] = one[t]
        weight_two[0:width, t * LANES : t * LANES + width] = two[TAPS - 1 - t]
    spread_a[...] = jnp.zeros_like(spread_a)
    spread_g[...] = jnp.zeros_like(spread_g)

    def widen(arrived, start, rim):
        value = arrived[start : start + rim_rows, :].astype(F32)
        rim[0:blocks] = value.reshape(blocks, 8, 8, LANES)
        rim[blocks] = jnp.zeros((8, 8, LANES), F32)

    rims_here(0)
    for kind, low, high in ((0, low_a, high_a), (1, low_g, high_g)):
        widen(land_low, kind * rim_rows, low)
        widen(land_high, kind * rim_rows, high)

    refs = (terms, stage, landing, whole, send_sem, recv_sem)
    streams = [
        Stream(i, i * stream_rows, stream_rows, orders[i % 2], place, refs) for i in range(4)
    ]

    def conv(cols, weight, b):
        y = jnp.zeros((span, LANES), F32)
        for dx in range(3):
            y += jnp.dot(
                cols[b, dx * PLANE : dx * PLANE + span, :],
                weight[dx * taps : (dx + 1) * taps, :],
                preferred_element_type=F32,
            )
        return y

    def outer(spread, cols):
        sums = None
        for b in range(blocks):
            part = lax.dot_general(
                spread[b], cols[b], (((0,), (0,)), ((), ())), preferred_element_type=F32
            )
            sums = part if sums is None else sums + part
        return sums

    build_windows(blocks, local_a, low_a, high_a, near, q, cols_a)
    zs = []
    for b in range(blocks):
        here = slice(b * span, (b + 1) * span)
        z = conv(cols_a, weight_one, b) * mask[here]
        zs.append(z)
        hidden = (z * (1.0 / (1.0 + jnp.exp(-z)))).astype(BF16)
        hidden_first[b * PLANE : (b + 1) * PLANE, :] = hidden[0:PLANE]
        hidden_last[b * PLANE : (b + 1) * PLANE, :] = hidden[span - PLANE : span]
        local_a[b] = hidden.astype(F32).reshape(8, 8, 8, LANES)
        for dx in range(3):
            rows = slice(dx * PLANE, dx * PLANE + span)
            spread_a[b, rows, dx * LANES : (dx + 1) * LANES] = hidden
    rims_go(2)

    build_windows(blocks, local_g, low_g, high_g, near, q, cols_g)
    sums = outer(spread_a, cols_g)

    def second_matrix(j):
        dx, k = (TAPS - 1 - j) // 9, (TAPS - 1 - j) % 9
        return sums[dx * LANES : dx * LANES + width, k * LANES : (k + 1) * LANES]

    fold(terms, 0, 2 * stream_rows, width, second_matrix)
    for stream in streams[:2]:
        stream.start()

    for b in range(blocks):
        ga = jnp.zeros((span, LANES), F32)
        for dx in range(3):
            ga += lax.dot_general(
                cols_g[b, dx * PLANE : dx * PLANE + span, :],
                weight_two[:, dx * taps : (dx + 1) * taps],
                (((1,), (1,)), ((), ())),
                preferred_element_type=F32,
            )
        z = zs[b]
        ga = ga * mask[b * span : (b + 1) * span]
        sigma = 1.0 / (1.0 + jnp.exp(-z))
        gz = (ga * sigma * (1.0 + z * (1.0 - sigma))).astype(BF16)
        for dx in range(3):
            rows = slice(dx * PLANE, dx * PLANE + span)
            spread_g[b, rows, dx * LANES : (dx + 1) * LANES] = gz
    for stream in streams[:2]:
        stream.advance()
    crossed = outer(spread_g, cols_a)

    def first_matrix(j):
        dx, k = j // 9, j % 9
        return crossed[dx * LANES : (dx + 1) * LANES, k * LANES : (k + 1) * LANES].T[0:width]

    fold(terms, 2 * stream_rows, 2 * stream_rows, width, first_matrix)
    for stream in streams[2:]:
        stream.start()
    for stream in streams[:2]:
        stream.advance()

    rims_here(2)
    widen(hidden_low, 0, low_a)
    widen(hidden_high, 0, high_a)
    for t in range(TAPS):
        weight_one[t * LANES : t * LANES + width, 0:width] = two[t]
    build_windows(blocks, local_a, low_a, high_a, near, q, cols_a)
    for stream in streams:
        stream.advance()
    for b in range(blocks):
        here = slice(b * span, (b + 1) * span)
        y = conv(cols_a, weight_one, b)
        out[:, here] = (y.T[0:width] * mask_row[:, here]).astype(BF16)
        for stream in streams:
            stream.advance()
    while not all(stream.done() for stream in streams):
        for stream in streams:
            stream.advance()
    for stream in streams:
        stream.close()
    rims_gone(0)
    rims_gone(2)
    total[...] = whole[...]


def unfold_kernel(width, scale, total, grad_one, grad_two):
    main, folded = fold_counts(width)
    each = main // folded
    half = total.shape[0] // 2
    for start, grad in ((0, grad_two), (half, grad_one)):

        def rows(place):
            at = start + place * width
            return total[at : at + width, :].astype(F32) * scale

        for group in range(folded):
            spare = []
            for chunk in range(each):
                value = rows(group * each + chunk)
                grad[group * each + chunk] = value[:, 0:width]
                spare.append(value[:, width:LANES])
            grad[main + group] = jnp.concatenate(spare, axis=1)
        for j in range(main + folded, TAPS):
            grad[j] = rows(j - folded)[:, 0:width]


def phases_of(axis, size, first):
    bits = size.bit_length() - 1
    phases = []
    while first < bits:
        step = min(2, bits - first)
        phases.append((axis, first, 1 << step))
        first += step
    return phases


def per_device(sizes, features_in, occupancy, cotangent, kernel_one, kernel_two, neighbours):
    width, voxels = features_in.shape
    blocks = neighbours.shape[0]
    devices = math.prod(sizes.values())
    scale = float(voxels * devices) ** (-0.5)
    vmem = pl.BlockSpec(memory_space=pltpu.VMEM)
    smem = pl.BlockSpec(memory_space=pltpu.SMEM)
    limit = 56 * 1024 * 1024

    core = [("group", 0, 2)]
    beside = [("dev", 0, 2)]
    across = phases_of("group", sizes["group"], 1)
    along = phases_of("dev", sizes["dev"], 1)
    orders = [core + beside + across + along, core + across + beside + along]
    slots = 2 * sum(radix - 1 for _, _, radix in orders[0])
    _, folded = fold_counts(width)
    used = (TAPS - folded) * width
    unit = 16 * devices
    stream_rows = -(-used // (2 * unit)) * unit
    rows = 4 * stream_rows

    rim = pltpu.VMEM((blocks + 1, 8, 8, LANES), F32)
    cube = pltpu.VMEM((blocks + 1, 8, 8, 8, LANES), F32)
    cols = pltpu.VMEM((blocks, 10 * PLANE, 9 * LANES), BF16)
    spread = pltpu.VMEM((blocks, 10 * PLANE, 3 * LANES), BF16)
    both_rims = pltpu.VMEM((2 * blocks * PLANE, LANES), BF16)
    one_rim = pltpu.VMEM((blocks * PLANE, LANES), BF16)
    packed = pltpu.VMEM((rows, LANES), BF16)
    out, total = pl.pallas_call(
        functools.partial(step_kernel, blocks, width, sizes, orders, stream_rows),
        out_shape=(
            jax.ShapeDtypeStruct((width, voxels), BF16),
            jax.ShapeDtypeStruct((rows, LANES), BF16),
        ),
        in_specs=[vmem] * 5 + [smem],
        out_specs=[vmem] * 2,
        scratch_shapes=[cube, cube, rim, rim, rim, rim]
        + [pltpu.VMEM((3, blocks, 10, 10, 8, LANES), F32), cols, cols]
        + [pltpu.VMEM((TAPS * LANES, LANES), BF16), pltpu.VMEM((LANES, TAPS * LANES), BF16)]
        + [spread, spread]
        + [both_rims] * 4
        + [one_rim] * 4
        + [pltpu.VMEM((rows, LANES), F32), packed, packed, packed]
        + [pltpu.SemaphoreType.DMA((4, slots))] * 2
        + [pltpu.SemaphoreType.DMA((4,))] * 2,
        compiler_params=pltpu.CompilerParams(
            collective_id=0, has_side_effects=True, vmem_limit_bytes=limit
        ),
        name="train_step",
    )(features_in, cotangent, occupancy[None, :], kernel_one, kernel_two, neighbours)
    grad_one, grad_two = pl.pallas_call(
        functools.partial(unfold_kernel, width, scale),
        out_shape=(jax.ShapeDtypeStruct((TAPS, width, width), F32),) * 2,
        in_specs=[vmem],
        out_specs=[vmem] * 2,
        compiler_params=pltpu.CompilerParams(vmem_limit_bytes=limit),
        name="unfold",
    )(total)
    return out, grad_one, grad_two


def solution(mesh):
    sizes = dict(mesh.shape)
    return jax.shard_map(
        functools.partial(per_device, sizes),
        mesh=mesh,
        in_specs=(
            P(None, ("group", "dev")),
            P(("group", "dev")),
            P(None, ("group", "dev")),
            P(),
            P(),
            P(("group", "dev"), None),
        ),
        out_specs=(P(None, ("group", "dev")), P(), P()),
        check_vma=False,
    )
```

```python
import functools
import math

import jax
import jax.numpy as jnp
from jax import lax
from jax.experimental import pallas as pl
from jax.experimental.pallas import tpu as pltpu
from jax.sharding import PartitionSpec as P

LANES = 128
TAPS = 27
PLANE = 64
F32 = jnp.float32
BF16 = jnp.bfloat16


def build_windows(blocks, local, lower, upper, near, q, cols, inner):
    row = lax.broadcasted_iota(jnp.int32, (1, 8, LANES), 1)

    def shifted(main, before, after):
        down = jnp.where(row == 0, pltpu.roll(before, 1, 1), pltpu.roll(main, 1, 1))
        up = jnp.where(row == 7, pltpu.roll(after, 7, 1), pltpu.roll(main, 7, 1))
        return down, main, up

    for b in range(blocks):
        for tx in (1,) if inner else (0, 2):
            for ty in range(3):
                src_y = (slice(7, 8), slice(0, 8), slice(0, 1))[ty]
                dst_y = (slice(0, 1), slice(1, 9), slice(9, 10))[ty]
                dst_x = (slice(0, 1), slice(1, 9), slice(9, 10))[tx]
                rows_y = src_y.stop - src_y.start
                rows_x = dst_x.stop - dst_x.start
                parts = []
                for tz in range(3):
                    n = near[b, tx * 9 + ty * 3 + tz]
                    n = n - (blocks, 0, 2 * blocks)[tx]
                    index = jnp.where((n >= 0) & (n < blocks), n, blocks)
                    if tx == 1:
                        value = local[index, :, src_y]
                    else:
                        value = (lower, None, upper)[tx][index, src_y]
                    parts.append(value.reshape(rows_x * rows_y, 8, LANES))
                moved = shifted(parts[1], parts[0], parts[2])
                for dz in range(3):
                    q[dz, b, dst_x, dst_y] = moved[dz].reshape(rows_x, rows_y, 8, LANES)
        for dy in range(3):
            for dz in range(3):
                k = dy * 3 + dz
                for x, end in ((1, 9),) if inner else ((0, 1), (9, 10)):
                    window = q[dz, b, x:end, dy : dy + 8].reshape((end - x) * PLANE, LANES)
                    lanes = slice(k * LANES, (k + 1) * LANES)
                    cols[b, x * PLANE : end * PLANE, lanes] = window.astype(BF16)


def tall(values, width):
    values = values.astype(F32)
    filler = jnp.zeros((LANES - width, values.shape[1]), F32)
    return jnp.concatenate([values, filler], axis=0).T


def fold_counts(width):
    each = width // (LANES - width)
    folded = TAPS // (each + 1)
    return folded * each, folded


def fold(terms, start, rows, width, matrix):
    main, folded = fold_counts(width)
    lane = lax.broadcasted_iota(jnp.int32, (width, LANES), 1)
    room = LANES - width
    each = width // room
    for j in range(main):
        chunk = j % each
        extra = pltpu.roll(matrix(main + j // each), (width - room * chunk) % LANES, 1)
        at = start + j * width
        terms[at : at + width, :] = jnp.where(lane < width, matrix(j), extra)
    for j in range(main + folded, TAPS):
        at = start + (j - folded) * width
        terms[at : at + width, :] = matrix(j)
    used = (TAPS - folded) * width
    terms[start + used : start + rows, :] = jnp.zeros((rows - used, LANES), F32)


class Stream:
    def __init__(self, number, start, rows, order, place, refs):
        self.number, self.base, self.length, self.order = number, start, rows, order
        self.at = start
        self.place = place
        self.terms, self.stage, self.landing, self.whole, self.send_sem, self.recv_sem = refs
        self.step = 0
        self.copies = []
        self.sent = []
        self.slot = 0

    def ds(self, start, size):
        return pl.ds(pl.multiple_of(start, 16), size)

    def send(self, src, dst, axis, other):
        copy = pltpu.make_async_remote_copy(
            src_ref=src,
            dst_ref=dst,
            send_sem=self.send_sem.at[self.number, self.slot],
            recv_sem=self.recv_sem.at[self.number, self.slot],
            device_id={axis: other},
            device_id_type=pl.DeviceIdType.MESH,
        )
        copy.start()
        self.slot += 1
        self.copies.append(copy)
        self.sent.append(copy)

    def start(self):
        count = len(self.order)
        self.copies = []
        if self.step < count:
            axis, low, radix = self.order[self.step]
            digit, others = peers(self.place, axis, low, radix)
            chunk = self.length // radix
            self.slots = []
            for theirs, other in others:
                here = slice(self.at, self.at + chunk)
                values = self.terms[self.ds(self.base + theirs * chunk, chunk), :]
                self.stage[here, :] = values.astype(BF16)
                rows = pl.ds(self.at, chunk)
                self.send(self.stage.at[rows], self.landing.at[rows], axis, other)
                self.slots.append(here)
                self.at += chunk
        else:
            axis, low, radix = self.order[2 * count - 1 - self.step]
            _, others = peers(self.place, axis, low, radix)
            here = self.whole.at[self.ds(self.base, self.length)]
            for _, other in others:
                self.send(here, here, axis, other)

    def finish(self):
        count = len(self.order)
        for copy in self.copies:
            copy.wait_recv()
        if self.step < count:
            axis, low, radix = self.order[self.step]
            digit, _ = peers(self.place, axis, low, radix)
            chunk = self.length // radix
            keep = self.base + digit * chunk
            value = self.terms[self.ds(keep, chunk), :]
            for here in self.slots:
                value = value + self.landing[here, :].astype(F32)
            if self.step == count - 1:
                self.whole[self.ds(keep, chunk), :] = value.astype(BF16)
            else:
                self.terms[self.ds(keep, chunk), :] = value
            self.base, self.length = keep, chunk
        else:
            axis, low, radix = self.order[2 * count - 1 - self.step]
            digit, _ = peers(self.place, axis, low, radix)
            self.base = self.base - digit * self.length
            self.length *= radix
        self.step += 1

    def done(self):
        return self.step == 2 * len(self.order)

    def advance(self):
        if not self.done():
            self.finish()
            if not self.done():
                self.start()

    def close(self):
        for copy in self.sent:
            copy.wait_send()


def peers(place, axis, low, radix):
    unit = 1 << low
    digit = (place[axis] // unit) % radix
    others = []
    for step in range(1, radix):
        theirs = (digit + step) % radix
        others.append((theirs, place[axis] + (theirs - digit) * unit))
    return digit, others


def step_kernel(
    blocks, width, sizes, orders, stream_rows,
    feat_far, cot_far, one_far, two_far, occ, near,
    out, total,
    feat, cot, one, two, in_sem, part_z, part_g,
    local_a, local_g, low_a, high_a, low_g, high_g, q, cols_a, cols_g, weight_one, weight_two,
    spread_a, spread_g, send_first, send_last, land_low, land_high,
    hidden_first, hidden_last, hidden_low, hidden_high,
    terms, stage, landing, whole, send_sem, recv_sem, rim_send, rim_recv,
):
    taps = 9 * LANES
    span = 8 * PLANE
    rim_rows = blocks * PLANE
    place = {axis: lax.axis_index(axis) for axis in sizes}
    dev, count = place["dev"], sizes["dev"]
    has_low = dev > 0
    has_high = dev < count - 1
    low_dev = (dev + count - 1) % count
    high_dev = (dev + 1) % count

    loads = [
        pltpu.make_async_copy(src, dst, in_sem.at[i])
        for i, (src, dst) in enumerate(
            ((feat_far, feat), (cot_far, cot), (one_far, one), (two_far, two))
        )
    ]
    for load in loads:
        load.start()
    for ref in (land_low, land_high, hidden_low, hidden_high):
        ref[...] = jnp.zeros_like(ref)

    barrier = pltpu.get_barrier_semaphore()

    def greet(axis, other):
        pl.semaphore_signal(
            barrier, inc=1, device_id={axis: other}, device_id_type=pl.DeviceIdType.MESH
        )

    greeted = 0
    for phase in orders[0]:
        for _, other in peers(place, *phase)[1]:
            greet(phase[0], other)
            greeted += 1

    @pl.when(has_low)
    def _():
        greet("dev", low_dev)

    @pl.when(has_high)
    def _():
        greet("dev", high_dev)

    def rim_copy(which, src, dst, other):
        return pltpu.make_async_remote_copy(
            src_ref=src,
            dst_ref=dst,
            send_sem=rim_send.at[which],
            recv_sem=rim_recv.at[which],
            device_id={"dev": other},
            device_id_type=pl.DeviceIdType.MESH,
        )

    rim_copies = [
        rim_copy(0, send_last, land_low, high_dev),
        rim_copy(1, send_first, land_high, low_dev),
        rim_copy(2, hidden_last, hidden_low, high_dev),
        rim_copy(3, hidden_first, hidden_high, low_dev),
    ]

    def rims_go(first):
        @pl.when(has_high)
        def _():
            rim_copies[first].start()

        @pl.when(has_low)
        def _():
            rim_copies[first + 1].start()

    def rims_here(first):
        @pl.when(has_low)
        def _():
            rim_copies[first].wait_recv()

        @pl.when(has_high)
        def _():
            rim_copies[first + 1].wait_recv()

    def rims_gone(first):
        @pl.when(has_high)
        def _():
            rim_copies[first].wait_send()

        @pl.when(has_low)
        def _():
            rim_copies[first + 1].wait_send()

    mask_row = (occ[...] > 0).astype(F32)
    loads[0].wait()
    loads[1].wait()
    for kind, source, local in ((0, feat, local_a), (1, cot, local_g)):
        value = tall(source[...].astype(F32) * mask_row, width)
        local[0:blocks] = value.reshape(blocks, 8, 8, 8, LANES)
        local[blocks] = jnp.zeros((8, 8, 8, LANES), F32)
        for b in range(blocks):
            at = kind * rim_rows + b * PLANE
            send_first[at : at + PLANE, :] = value[b * span : b * span + PLANE].astype(BF16)
            send_last[at : at + PLANE, :] = value[(b + 1) * span - PLANE : (b + 1) * span].astype(BF16)

    pl.semaphore_wait(barrier, greeted + has_low.astype(jnp.int32) + has_high.astype(jnp.int32))
    rims_go(0)

    mask = jnp.broadcast_to(mask_row, (LANES, blocks * span)).T
    weight_one[...] = jnp.zeros_like(weight_one)
    weight_two[...] = jnp.zeros_like(weight_two)
    loads[2].wait()
    loads[3].wait()
    for t in range(TAPS):
        weight_one[t * LANES : t * LANES + width, 0:width] = one[t]
        weight_two[0:width, t * LANES : t * LANES + width] = two[TAPS - 1 - t]
    spread_a[...] = jnp.zeros_like(spread_a)
    spread_g[...] = jnp.zeros_like(spread_g)

    def widen(arrived, start, rim):
        value = arrived[start : start + rim_rows, :].astype(F32)
        rim[0:blocks] = value.reshape(blocks, 8, 8, LANES)
        rim[blocks] = jnp.zeros((8, 8, LANES), F32)

    def conv(cols, weight, b, steps):
        y = None
        for dx in steps:
            term = jnp.dot(
                cols[b, dx * PLANE : dx * PLANE + span, :],
                weight[dx * taps : (dx + 1) * taps, :],
                preferred_element_type=F32,
            )
            y = term if y is None else y + term
        return y

    def conv_back(b, steps):
        y = None
        for dx in steps:
            term = lax.dot_general(
                cols_g[b, dx * PLANE : dx * PLANE + span, :],
                weight_two[:, dx * taps : (dx + 1) * taps],
                (((1,), (1,)), ((), ())),
                preferred_element_type=F32,
            )
            y = term if y is None else y + term
        return y

    build_windows(blocks, local_a, low_a, high_a, near, q, cols_a, True)
    for b in range(blocks):
        part_z[b] = conv(cols_a, weight_one, b, (1,))
    build_windows(blocks, local_g, low_g, high_g, near, q, cols_g, True)
    for b in range(blocks):
        part_g[b] = conv_back(b, (1,))

    rims_here(0)
    for kind, low, high in ((0, low_a, high_a), (1, low_g, high_g)):
        widen(land_low, kind * rim_rows, low)
        widen(land_high, kind * rim_rows, high)

    refs = (terms, stage, landing, whole, send_sem, recv_sem)
    streams = [
        Stream(i, i * stream_rows, stream_rows, orders[i % 2], place, refs) for i in range(4)
    ]

    def outer(spread, cols):
        sums = None
        for b in range(blocks):
            part = lax.dot_general(
                spread[b], cols[b], (((0,), (0,)), ((), ())), preferred_element_type=F32
            )
            sums = part if sums is None else sums + part
        return sums

    build_windows(blocks, local_a, low_a, high_a, near, q, cols_a, False)
    zs = []
    for b in range(blocks):
        here = slice(b * span, (b + 1) * span)
        z = (part_z[b] + conv(cols_a, weight_one, b, (0, 2))) * mask[here]
        zs.append(z)
        hidden = (z * (1.0 / (1.0 + jnp.exp(-z)))).astype(BF16)
        hidden_first[b * PLANE : (b + 1) * PLANE, :] = hidden[0:PLANE]
        hidden_last[b * PLANE : (b + 1) * PLANE, :] = hidden[span - PLANE : span]
        local_a[b] = hidden.astype(F32).reshape(8, 8, 8, LANES)
        for dx in range(3):
            rows = slice(dx * PLANE, dx * PLANE + span)
            spread_a[b, rows, dx * LANES : (dx + 1) * LANES] = hidden
    rims_go(2)

    build_windows(blocks, local_g, low_g, high_g, near, q, cols_g, False)
    sums = outer(spread_a, cols_g)

    def second_matrix(j):
        dx, k = (TAPS - 1 - j) // 9, (TAPS - 1 - j) % 9
        return sums[dx * LANES : dx * LANES + width, k * LANES : (k + 1) * LANES]

    fold(terms, 0, 2 * stream_rows, width, second_matrix)
    for stream in streams[:2]:
        stream.start()

    for b in range(blocks):
        ga = part_g[b] + conv_back(b, (0, 2))
        z = zs[b]
        ga = ga * mask[b * span : (b + 1) * span]
        sigma = 1.0 / (1.0 + jnp.exp(-z))
        gz = (ga * sigma * (1.0 + z * (1.0 - sigma))).astype(BF16)
        for dx in range(3):
            rows = slice(dx * PLANE, dx * PLANE + span)
            spread_g[b, rows, dx * LANES : (dx + 1) * LANES] = gz
    for stream in streams[:2]:
        stream.advance()
    crossed = outer(spread_g, cols_a)

    def first_matrix(j):
        dx, k = j // 9, j % 9
        return crossed[dx * LANES : (dx + 1) * LANES, k * LANES : (k + 1) * LANES].T[0:width]

    fold(terms, 2 * stream_rows, 2 * stream_rows, width, first_matrix)
    for stream in streams[2:]:
        stream.start()
    for stream in streams[:2]:
        stream.advance()

    rims_here(2)
    widen(hidden_low, 0, low_a)
    widen(hidden_high, 0, high_a)
    for t in range(TAPS):
        weight_one[t * LANES : t * LANES + width, 0:width] = two[t]
    build_windows(blocks, local_a, low_a, high_a, near, q, cols_a, True)
    build_windows(blocks, local_a, low_a, high_a, near, q, cols_a, False)
    for stream in streams:
        stream.advance()
    for b in range(blocks):
        here = slice(b * span, (b + 1) * span)
        y = conv(cols_a, weight_one, b, (0, 1, 2))
        out[:, here] = (y.T[0:width] * mask_row[:, here]).astype(BF16)
        for stream in streams:
            stream.advance()
    while not all(stream.done() for stream in streams):
        for stream in streams:
            stream.advance()
    for stream in streams:
        stream.close()
    rims_gone(0)
    rims_gone(2)
    total[...] = whole[...]


def unfold_kernel(width, scale, total, features, out, grad_one, grad_two):
    out[...] = features[...]
    main, folded = fold_counts(width)
    each = main // folded
    half = total.shape[0] // 2
    for start, grad in ((0, grad_two), (half, grad_one)):

        def rows(place):
            at = start + place * width
            return total[at : at + width, :].astype(F32) * scale

        for group in range(folded):
            spare = []
            for chunk in range(each):
                value = rows(group * each + chunk)
                grad[group * each + chunk] = value[:, 0:width]
                spare.append(value[:, width:LANES])
            grad[main + group] = jnp.concatenate(spare, axis=1)
        for j in range(main + folded, TAPS):
            grad[j] = rows(j - folded)[:, 0:width]


def phases_of(axis, size, first):
    bits = size.bit_length() - 1
    phases = []
    while first < bits:
        step = min(2, bits - first)
        phases.append((axis, first, 1 << step))
        first += step
    return phases


def per_device(sizes, features_in, occupancy, cotangent, kernel_one, kernel_two, neighbours):
    width, voxels = features_in.shape
    blocks = neighbours.shape[0]
    devices = math.prod(sizes.values())
    scale = float(voxels * devices) ** (-0.5)
    vmem = pl.BlockSpec(memory_space=pltpu.VMEM)
    smem = pl.BlockSpec(memory_space=pltpu.SMEM)
    limit = 56 * 1024 * 1024

    core = [("group", 0, 2)]
    beside = [("dev", 0, 2)]
    across = phases_of("group", sizes["group"], 1)
    along = phases_of("dev", sizes["dev"], 1)
    orders = [core + beside + across + along, core + across + beside + along]
    slots = 2 * sum(radix - 1 for _, _, radix in orders[0])
    _, folded = fold_counts(width)
    used = (TAPS - folded) * width
    unit = 16 * devices
    stream_rows = -(-used // (2 * unit)) * unit
    rows = 4 * stream_rows

    rim = pltpu.VMEM((blocks + 1, 8, 8, LANES), F32)
    cube = pltpu.VMEM((blocks + 1, 8, 8, 8, LANES), F32)
    cols = pltpu.VMEM((blocks, 10 * PLANE, 9 * LANES), BF16)
    spread = pltpu.VMEM((blocks, 10 * PLANE, 3 * LANES), BF16)
    both_rims = pltpu.VMEM((2 * blocks * PLANE, LANES), BF16)
    one_rim = pltpu.VMEM((blocks * PLANE, LANES), BF16)
    packed = pltpu.VMEM((rows, LANES), BF16)
    features, total = pl.pallas_call(
        functools.partial(step_kernel, blocks, width, sizes, orders, stream_rows),
        out_shape=(
            jax.ShapeDtypeStruct((width, voxels), BF16),
            jax.ShapeDtypeStruct((rows, LANES), BF16),
        ),
        in_specs=[pl.BlockSpec(memory_space=pl.ANY)] * 4 + [vmem, smem],
        out_specs=[vmem] * 2,
        scratch_shapes=[pltpu.VMEM((width, voxels), BF16)] * 2
        + [pltpu.VMEM((TAPS, width, width), BF16)] * 2
        + [pltpu.SemaphoreType.DMA((4,))]
        + [pltpu.VMEM((blocks, 8 * PLANE, LANES), F32)] * 2
        + [cube, cube, rim, rim, rim, rim]
        + [pltpu.VMEM((3, blocks, 10, 10, 8, LANES), F32), cols, cols]
        + [pltpu.VMEM((TAPS * LANES, LANES), BF16), pltpu.VMEM((LANES, TAPS * LANES), BF16)]
        + [spread, spread]
        + [both_rims] * 4
        + [one_rim] * 4
        + [pltpu.VMEM((rows, LANES), F32), packed, packed, packed]
        + [pltpu.SemaphoreType.DMA((4, slots))] * 2
        + [pltpu.SemaphoreType.DMA((4,))] * 2,
        compiler_params=pltpu.CompilerParams(
            collective_id=0, has_side_effects=True, vmem_limit_bytes=limit
        ),
        name="train_step",
    )(features_in, cotangent, kernel_one, kernel_two, occupancy[None, :], neighbours)
    return pl.pallas_call(
        functools.partial(unfold_kernel, width, scale),
        out_shape=(
            jax.ShapeDtypeStruct((width, voxels), BF16),
            jax.ShapeDtypeStruct((TAPS, width, width), F32),
            jax.ShapeDtypeStruct((TAPS, width, width), F32),
        ),
        in_specs=[vmem] * 2,
        out_specs=[vmem] * 3,
        compiler_params=pltpu.CompilerParams(vmem_limit_bytes=16 * 1024 * 1024),
        name="unfold",
    )(total, features)


def solution(mesh):
    sizes = dict(mesh.shape)
    return jax.shard_map(
        functools.partial(per_device, sizes),
        mesh=mesh,
        in_specs=(
            P(None, ("group", "dev")),
            P(("group", "dev")),
            P(None, ("group", "dev")),
            P(),
            P(),
            P(("group", "dev"), None),
        ),
        out_specs=(P(None, ("group", "dev")), P(), P()),
        check_vma=False,
    )
```

```python
import functools
import math

import jax
import jax.numpy as jnp
from jax import lax
from jax.experimental import pallas as pl
from jax.experimental.pallas import tpu as pltpu
from jax.sharding import PartitionSpec as P

LANES = 128
TAPS = 27
PLANE = 64
F32 = jnp.float32
BF16 = jnp.bfloat16


def build_windows(blocks, local, lower, upper, near, q, cols, inner):
    row = lax.broadcasted_iota(jnp.int32, (1, 8, LANES), 1)

    def shifted(main, before, after):
        down = jnp.where(row == 0, pltpu.roll(before, 1, 1), pltpu.roll(main, 1, 1))
        up = jnp.where(row == 7, pltpu.roll(after, 7, 1), pltpu.roll(main, 7, 1))
        return down, main, up

    for b in range(blocks):
        for tx in (1,) if inner else (0, 2):
            for ty in range(3):
                src_y = (slice(7, 8), slice(0, 8), slice(0, 1))[ty]
                dst_y = (slice(0, 1), slice(1, 9), slice(9, 10))[ty]
                dst_x = (slice(0, 1), slice(1, 9), slice(9, 10))[tx]
                rows_y = src_y.stop - src_y.start
                rows_x = dst_x.stop - dst_x.start
                parts = []
                for tz in range(3):
                    n = near[b, tx * 9 + ty * 3 + tz]
                    n = n - (blocks, 0, 2 * blocks)[tx]
                    index = jnp.where((n >= 0) & (n < blocks), n, blocks)
                    if tx == 1:
                        value = local[index, :, src_y]
                    else:
                        value = (lower, None, upper)[tx][index, src_y]
                    parts.append(value.reshape(rows_x * rows_y, 8, LANES))
                moved = shifted(parts[1], parts[0], parts[2])
                for dz in range(3):
                    q[dz, b, dst_x, dst_y] = moved[dz].reshape(rows_x, rows_y, 8, LANES)
        for dy in range(3):
            for dz in range(3):
                k = dy * 3 + dz
                for x, end in ((1, 9),) if inner else ((0, 1), (9, 10)):
                    window = q[dz, b, x:end, dy : dy + 8].reshape((end - x) * PLANE, LANES)
                    lanes = slice(k * LANES, (k + 1) * LANES)
                    cols[b, x * PLANE : end * PLANE, lanes] = window.astype(BF16)


def tall(values, width):
    values = values.astype(F32)
    filler = jnp.zeros((LANES - width, values.shape[1]), F32)
    return jnp.concatenate([values, filler], axis=0).T


def fold_counts(width):
    each = width // (LANES - width)
    folded = TAPS // (each + 1)
    return folded * each, folded


def fold(terms, start, rows, width, matrix):
    main, folded = fold_counts(width)
    lane = lax.broadcasted_iota(jnp.int32, (width, LANES), 1)
    room = LANES - width
    each = width // room
    for j in range(main):
        chunk = j % each
        extra = pltpu.roll(matrix(main + j // each), (width - room * chunk) % LANES, 1)
        at = start + j * width
        terms[at : at + width, :] = jnp.where(lane < width, matrix(j), extra)
    for j in range(main + folded, TAPS):
        at = start + (j - folded) * width
        terms[at : at + width, :] = matrix(j)
    used = (TAPS - folded) * width
    terms[start + used : start + rows, :] = jnp.zeros((rows - used, LANES), F32)


class Stream:
    def __init__(self, number, start, rows, order, place, refs):
        self.number, self.base, self.length, self.order = number, start, rows, order
        self.at = start
        self.place = place
        self.terms, self.stage, self.landing, self.whole, self.send_sem, self.recv_sem = refs
        self.step = 0
        self.copies = []
        self.sent = []
        self.slot = 0

    def ds(self, start, size):
        return pl.ds(pl.multiple_of(start, 16), size)

    def send(self, src, dst, axis, other):
        copy = pltpu.make_async_remote_copy(
            src_ref=src,
            dst_ref=dst,
            send_sem=self.send_sem.at[self.number, self.slot],
            recv_sem=self.recv_sem.at[self.number, self.slot],
            device_id={axis: other},
            device_id_type=pl.DeviceIdType.MESH,
        )
        copy.start()
        self.slot += 1
        self.copies.append(copy)
        self.sent.append(copy)

    def start(self):
        count = len(self.order)
        self.copies = []
        if self.step < count:
            axis, low, radix = self.order[self.step]
            digit, others = peers(self.place, axis, low, radix)
            chunk = self.length // radix
            self.slots = []
            for theirs, other in others:
                here = slice(self.at, self.at + chunk)
                values = self.terms[self.ds(self.base + theirs * chunk, chunk), :]
                self.stage[here, :] = values.astype(BF16)
                rows = pl.ds(self.at, chunk)
                self.send(self.stage.at[rows], self.landing.at[rows], axis, other)
                self.slots.append(here)
                self.at += chunk
        else:
            axis, low, radix = self.order[2 * count - 1 - self.step]
            _, others = peers(self.place, axis, low, radix)
            here = self.whole.at[self.ds(self.base, self.length)]
            for _, other in others:
                self.send(here, here, axis, other)

    def finish(self):
        count = len(self.order)
        for copy in self.copies:
            copy.wait_recv()
        if self.step < count:
            axis, low, radix = self.order[self.step]
            digit, _ = peers(self.place, axis, low, radix)
            chunk = self.length // radix
            keep = self.base + digit * chunk
            value = self.terms[self.ds(keep, chunk), :]
            for here in self.slots:
                value = value + self.landing[here, :].astype(F32)
            if self.step == count - 1:
                self.whole[self.ds(keep, chunk), :] = value.astype(BF16)
            else:
                self.terms[self.ds(keep, chunk), :] = value
            self.base, self.length = keep, chunk
        else:
            axis, low, radix = self.order[2 * count - 1 - self.step]
            digit, _ = peers(self.place, axis, low, radix)
            self.base = self.base - digit * self.length
            self.length *= radix
        self.step += 1

    def done(self):
        return self.step == 2 * len(self.order)

    def advance(self):
        if not self.done():
            self.finish()
            if not self.done():
                self.start()

    def close(self):
        for copy in self.sent:
            copy.wait_send()


def peers(place, axis, low, radix):
    unit = 1 << low
    digit = (place[axis] // unit) % radix
    others = []
    for step in range(1, radix):
        theirs = (digit + step) % radix
        others.append((theirs, place[axis] + (theirs - digit) * unit))
    return digit, others


def step_kernel(
    blocks, width, sizes, orders, stream_rows,
    feat_far, cot_far, one_far, two_far, occ, near,
    out_far, total_far,
    out, out_sem, feat, cot, one, two, in_sem, part_z, part_g,
    local_a, local_g, low_a, high_a, low_g, high_g, q, cols_a, cols_g, weight_one, weight_two,
    spread_a, spread_g, send_first, send_last, land_low, land_high,
    hidden_first, hidden_last, hidden_low, hidden_high,
    terms, stage, landing, whole, send_sem, recv_sem, rim_send, rim_recv,
):
    taps = 9 * LANES
    span = 8 * PLANE
    rim_rows = blocks * PLANE
    place = {axis: lax.axis_index(axis) for axis in sizes}
    dev, count = place["dev"], sizes["dev"]
    has_low = dev > 0
    has_high = dev < count - 1
    low_dev = (dev + count - 1) % count
    high_dev = (dev + 1) % count

    loads = [
        pltpu.make_async_copy(src, dst, in_sem.at[i])
        for i, (src, dst) in enumerate(
            ((feat_far, feat), (cot_far, cot), (one_far, one), (two_far, two))
        )
    ]
    for load in loads:
        load.start()
    for ref in (land_low, land_high, hidden_low, hidden_high):
        ref[...] = jnp.zeros_like(ref)

    barrier = pltpu.get_barrier_semaphore()

    def greet(axis, other):
        pl.semaphore_signal(
            barrier, inc=1, device_id={axis: other}, device_id_type=pl.DeviceIdType.MESH
        )

    greeted = 0
    for phase in orders[0]:
        for _, other in peers(place, *phase)[1]:
            greet(phase[0], other)
            greeted += 1

    @pl.when(has_low)
    def _():
        greet("dev", low_dev)

    @pl.when(has_high)
    def _():
        greet("dev", high_dev)

    def rim_copy(which, src, dst, other):
        return pltpu.make_async_remote_copy(
            src_ref=src,
            dst_ref=dst,
            send_sem=rim_send.at[which],
            recv_sem=rim_recv.at[which],
            device_id={"dev": other},
            device_id_type=pl.DeviceIdType.MESH,
        )

    rim_copies = [
        rim_copy(0, send_last, land_low, high_dev),
        rim_copy(1, send_first, land_high, low_dev),
        rim_copy(2, hidden_last, hidden_low, high_dev),
        rim_copy(3, hidden_first, hidden_high, low_dev),
    ]

    def rims_go(first):
        @pl.when(has_high)
        def _():
            rim_copies[first].start()

        @pl.when(has_low)
        def _():
            rim_copies[first + 1].start()

    def rims_here(first):
        @pl.when(has_low)
        def _():
            rim_copies[first].wait_recv()

        @pl.when(has_high)
        def _():
            rim_copies[first + 1].wait_recv()

    def rims_gone(first):
        @pl.when(has_high)
        def _():
            rim_copies[first].wait_send()

        @pl.when(has_low)
        def _():
            rim_copies[first + 1].wait_send()

    mask_row = (occ[...] > 0).astype(F32)
    loads[0].wait()
    loads[1].wait()
    for kind, source, local in ((0, feat, local_a), (1, cot, local_g)):
        value = tall(source[...].astype(F32) * mask_row, width)
        local[0:blocks] = value.reshape(blocks, 8, 8, 8, LANES)
        local[blocks] = jnp.zeros((8, 8, 8, LANES), F32)
        for b in range(blocks):
            at = kind * rim_rows + b * PLANE
            send_first[at : at + PLANE, :] = value[b * span : b * span + PLANE].astype(BF16)
            send_last[at : at + PLANE, :] = value[(b + 1) * span - PLANE : (b + 1) * span].astype(BF16)

    pl.semaphore_wait(barrier, greeted + has_low.astype(jnp.int32) + has_high.astype(jnp.int32))
    rims_go(0)

    mask = jnp.broadcast_to(mask_row, (LANES, blocks * span)).T
    weight_one[...] = jnp.zeros_like(weight_one)
    weight_two[...] = jnp.zeros_like(weight_two)
    loads[2].wait()
    loads[3].wait()
    for t in range(TAPS):
        weight_one[t * LANES : t * LANES + width, 0:width] = one[t]
        weight_two[0:width, t * LANES : t * LANES + width] = two[TAPS - 1 - t]
    spread_a[...] = jnp.zeros_like(spread_a)
    spread_g[...] = jnp.zeros_like(spread_g)

    def widen(arrived, start, rim):
        value = arrived[start : start + rim_rows, :].astype(F32)
        rim[0:blocks] = value.reshape(blocks, 8, 8, LANES)
        rim[blocks] = jnp.zeros((8, 8, LANES), F32)

    def conv(cols, weight, b, steps):
        y = None
        for dx in steps:
            term = jnp.dot(
                cols[b, dx * PLANE : dx * PLANE + span, :],
                weight[dx * taps : (dx + 1) * taps, :],
                preferred_element_type=F32,
            )
            y = term if y is None else y + term
        return y

    def conv_back(b, steps):
        y = None
        for dx in steps:
            term = lax.dot_general(
                cols_g[b, dx * PLANE : dx * PLANE + span, :],
                weight_two[:, dx * taps : (dx + 1) * taps],
                (((1,), (1,)), ((), ())),
                preferred_element_type=F32,
            )
            y = term if y is None else y + term
        return y

    build_windows(blocks, local_a, low_a, high_a, near, q, cols_a, True)
    for b in range(blocks):
        part_z[b] = conv(cols_a, weight_one, b, (1,))
    build_windows(blocks, local_g, low_g, high_g, near, q, cols_g, True)
    for b in range(blocks):
        part_g[b] = conv_back(b, (1,))

    rims_here(0)
    for kind, low, high in ((0, low_a, high_a), (1, low_g, high_g)):
        widen(land_low, kind * rim_rows, low)
        widen(land_high, kind * rim_rows, high)

    refs = (terms, stage, landing, whole, send_sem, recv_sem)
    streams = [
        Stream(i, i * stream_rows, stream_rows, orders[i % 2], place, refs) for i in range(4)
    ]

    def outer(spread, cols):
        sums = None
        for b in range(blocks):
            part = lax.dot_general(
                spread[b], cols[b], (((0,), (0,)), ((), ())), preferred_element_type=F32
            )
            sums = part if sums is None else sums + part
        return sums

    build_windows(blocks, local_a, low_a, high_a, near, q, cols_a, False)
    zs = []
    for b in range(blocks):
        here = slice(b * span, (b + 1) * span)
        z = (part_z[b] + conv(cols_a, weight_one, b, (0, 2))) * mask[here]
        zs.append(z)
        hidden = (z * (1.0 / (1.0 + jnp.exp(-z)))).astype(BF16)
        hidden_first[b * PLANE : (b + 1) * PLANE, :] = hidden[0:PLANE]
        hidden_last[b * PLANE : (b + 1) * PLANE, :] = hidden[span - PLANE : span]
        local_a[b] = hidden.astype(F32).reshape(8, 8, 8, LANES)
        for dx in range(3):
            rows = slice(dx * PLANE, dx * PLANE + span)
            spread_a[b, rows, dx * LANES : (dx + 1) * LANES] = hidden
    rims_go(2)

    build_windows(blocks, local_g, low_g, high_g, near, q, cols_g, False)
    sums = outer(spread_a, cols_g)

    def second_matrix(j):
        dx, k = (TAPS - 1 - j) // 9, (TAPS - 1 - j) % 9
        return sums[dx * LANES : dx * LANES + width, k * LANES : (k + 1) * LANES]

    fold(terms, 0, 2 * stream_rows, width, second_matrix)
    for stream in streams[:2]:
        stream.start()

    for b in range(blocks):
        ga = part_g[b] + conv_back(b, (0, 2))
        z = zs[b]
        ga = ga * mask[b * span : (b + 1) * span]
        sigma = 1.0 / (1.0 + jnp.exp(-z))
        gz = (ga * sigma * (1.0 + z * (1.0 - sigma))).astype(BF16)
        for dx in range(3):
            rows = slice(dx * PLANE, dx * PLANE + span)
            spread_g[b, rows, dx * LANES : (dx + 1) * LANES] = gz
    for stream in streams[:2]:
        stream.advance()
    crossed = outer(spread_g, cols_a)

    def first_matrix(j):
        dx, k = j // 9, j % 9
        return crossed[dx * LANES : (dx + 1) * LANES, k * LANES : (k + 1) * LANES].T[0:width]

    fold(terms, 2 * stream_rows, 2 * stream_rows, width, first_matrix)
    for stream in streams[2:]:
        stream.start()
    for stream in streams[:2]:
        stream.advance()

    rims_here(2)
    widen(hidden_low, 0, low_a)
    widen(hidden_high, 0, high_a)
    for t in range(TAPS):
        weight_one[t * LANES : t * LANES + width, 0:width] = two[t]
    build_windows(blocks, local_a, low_a, high_a, near, q, cols_a, True)
    build_windows(blocks, local_a, low_a, high_a, near, q, cols_a, False)
    for stream in streams:
        stream.advance()
    for b in range(blocks):
        here = slice(b * span, (b + 1) * span)
        y = conv(cols_a, weight_one, b, (0, 1, 2))
        out[:, here] = (y.T[0:width] * mask_row[:, here]).astype(BF16)
        for stream in streams:
            stream.advance()
    stores = [pltpu.make_async_copy(out, out_far, out_sem.at[0])]
    stores[0].start()

    def store_half(which):
        rows = pl.ds(which * 2 * stream_rows, 2 * stream_rows)
        store = pltpu.make_async_copy(whole.at[rows], total_far.at[rows], out_sem.at[1 + which])
        store.start()
        stores.append(store)

    while not all(stream.done() for stream in streams[:2]):
        for stream in streams:
            stream.advance()
    store_half(0)
    while not all(stream.done() for stream in streams):
        for stream in streams:
            stream.advance()
    store_half(1)
    for stream in streams:
        stream.close()
    rims_gone(0)
    rims_gone(2)
    for store in stores:
        store.wait()


def unfold_kernel(
    width, scale, total_far, features_far, out_far, one_far, two_far, total, grad_one, grad_two, sem
):
    main, folded = fold_counts(width)
    each = main // folded
    half = total.shape[0] // 2
    loads = [
        pltpu.make_async_copy(
            total_far.at[pl.ds(i * half, half)], total.at[pl.ds(i * half, half)], sem.at[i]
        )
        for i in range(2)
    ]
    stores = [pltpu.make_async_copy(features_far, out_far, sem.at[2])]
    for copy in loads + stores:
        copy.start()
    for i, grad, far in ((0, grad_two, two_far), (1, grad_one, one_far)):
        start = i * half
        loads[i].wait()

        def rows(place):
            at = start + place * width
            return total[at : at + width, :].astype(F32) * scale

        for group in range(folded):
            spare = []
            for chunk in range(each):
                value = rows(group * each + chunk)
                grad[group * each + chunk] = value[:, 0:width]
                spare.append(value[:, width:LANES])
            grad[main + group] = jnp.concatenate(spare, axis=1)
        for j in range(main + folded, TAPS):
            grad[j] = rows(j - folded)[:, 0:width]
        store = pltpu.make_async_copy(grad, far, sem.at[3 + i])
        store.start()
        stores.append(store)
    for store in stores:
        store.wait()


def phases_of(axis, size, first):
    bits = size.bit_length() - 1
    phases = []
    while first < bits:
        step = min(2, bits - first)
        phases.append((axis, first, 1 << step))
        first += step
    return phases


def per_device(sizes, features_in, occupancy, cotangent, kernel_one, kernel_two, neighbours):
    width, voxels = features_in.shape
    blocks = neighbours.shape[0]
    devices = math.prod(sizes.values())
    scale = float(voxels * devices) ** (-0.5)
    vmem = pl.BlockSpec(memory_space=pltpu.VMEM)
    smem = pl.BlockSpec(memory_space=pltpu.SMEM)
    limit = 56 * 1024 * 1024

    core = [("group", 0, 2)]
    beside = [("dev", 0, 2)]
    across = phases_of("group", sizes["group"], 1)
    along = phases_of("dev", sizes["dev"], 1)
    orders = [core + beside + across + along, core + across + beside + along]
    slots = 2 * sum(radix - 1 for _, _, radix in orders[0])
    _, folded = fold_counts(width)
    used = (TAPS - folded) * width
    unit = 16 * devices
    stream_rows = -(-used // (2 * unit)) * unit
    rows = 4 * stream_rows

    rim = pltpu.VMEM((blocks + 1, 8, 8, LANES), F32)
    cube = pltpu.VMEM((blocks + 1, 8, 8, 8, LANES), F32)
    cols = pltpu.VMEM((blocks, 10 * PLANE, 9 * LANES), BF16)
    spread = pltpu.VMEM((blocks, 10 * PLANE, 3 * LANES), BF16)
    both_rims = pltpu.VMEM((2 * blocks * PLANE, LANES), BF16)
    one_rim = pltpu.VMEM((blocks * PLANE, LANES), BF16)
    packed = pltpu.VMEM((rows, LANES), BF16)
    features, total = pl.pallas_call(
        functools.partial(step_kernel, blocks, width, sizes, orders, stream_rows),
        out_shape=(
            jax.ShapeDtypeStruct((width, voxels), BF16),
            jax.ShapeDtypeStruct((rows, LANES), BF16),
        ),
        in_specs=[pl.BlockSpec(memory_space=pl.ANY)] * 4 + [vmem, smem],
        out_specs=[pl.BlockSpec(memory_space=pl.ANY)] * 2,
        scratch_shapes=[pltpu.VMEM((width, voxels), BF16), pltpu.SemaphoreType.DMA((3,))]
        + [pltpu.VMEM((width, voxels), BF16)] * 2
        + [pltpu.VMEM((TAPS, width, width), BF16)] * 2
        + [pltpu.SemaphoreType.DMA((4,))]
        + [pltpu.VMEM((blocks, 8 * PLANE, LANES), F32)] * 2
        + [cube, cube, rim, rim, rim, rim]
        + [pltpu.VMEM((3, blocks, 10, 10, 8, LANES), F32), cols, cols]
        + [pltpu.VMEM((TAPS * LANES, LANES), BF16), pltpu.VMEM((LANES, TAPS * LANES), BF16)]
        + [spread, spread]
        + [both_rims] * 4
        + [one_rim] * 4
        + [pltpu.VMEM((rows, LANES), F32), packed, packed, packed]
        + [pltpu.SemaphoreType.DMA((4, slots))] * 2
        + [pltpu.SemaphoreType.DMA((4,))] * 2,
        compiler_params=pltpu.CompilerParams(
            collective_id=0, has_side_effects=True, vmem_limit_bytes=limit
        ),
        name="train_step",
    )(features_in, cotangent, kernel_one, kernel_two, occupancy[None, :], neighbours)
    return pl.pallas_call(
        functools.partial(unfold_kernel, width, scale),
        out_shape=(
            jax.ShapeDtypeStruct((width, voxels), BF16),
            jax.ShapeDtypeStruct((TAPS, width, width), F32),
            jax.ShapeDtypeStruct((TAPS, width, width), F32),
        ),
        in_specs=[pl.BlockSpec(memory_space=pl.ANY)] * 2,
        out_specs=[pl.BlockSpec(memory_space=pl.ANY)] * 3,
        scratch_shapes=[pltpu.VMEM((rows, LANES), BF16)]
        + [pltpu.VMEM((TAPS, width, width), F32)] * 2
        + [pltpu.SemaphoreType.DMA((5,))],
        compiler_params=pltpu.CompilerParams(vmem_limit_bytes=limit),
        name="unfold",
    )(total, features)


def solution(mesh):
    sizes = dict(mesh.shape)
    return jax.shard_map(
        functools.partial(per_device, sizes),
        mesh=mesh,
        in_specs=(
            P(None, ("group", "dev")),
            P(("group", "dev")),
            P(None, ("group", "dev")),
            P(),
            P(),
            P(("group", "dev"), None),
        ),
        out_specs=(P(None, ("group", "dev")), P(), P()),
        check_vma=False,
    )
```

```python
import functools
import math

import jax
import jax.numpy as jnp
from jax import lax
from jax.experimental import pallas as pl
from jax.experimental.pallas import tpu as pltpu
from jax.sharding import PartitionSpec as P

LANES = 128
TAPS = 27
PLANE = 64
F32 = jnp.float32
BF16 = jnp.bfloat16


def build_windows(blocks, local, lower, upper, near, q, cols, inner):
    row = lax.broadcasted_iota(jnp.int32, (1, 8, LANES), 1)

    def shifted(main, before, after):
        down = jnp.where(row == 0, pltpu.roll(before, 1, 1), pltpu.roll(main, 1, 1))
        up = jnp.where(row == 7, pltpu.roll(after, 7, 1), pltpu.roll(main, 7, 1))
        return down, main, up

    for b in range(blocks):
        for tx in (1,) if inner else (0, 2):
            for ty in range(3):
                src_y = (slice(7, 8), slice(0, 8), slice(0, 1))[ty]
                dst_y = (slice(0, 1), slice(1, 9), slice(9, 10))[ty]
                dst_x = (slice(0, 1), slice(1, 9), slice(9, 10))[tx]
                rows_y = src_y.stop - src_y.start
                rows_x = dst_x.stop - dst_x.start
                parts = []
                for tz in range(3):
                    n = near[b, tx * 9 + ty * 3 + tz]
                    n = n - (blocks, 0, 2 * blocks)[tx]
                    index = jnp.where((n >= 0) & (n < blocks), n, blocks)
                    if tx == 1:
                        value = local[index, :, src_y]
                    else:
                        value = (lower, None, upper)[tx][index, src_y]
                    parts.append(value.reshape(rows_x * rows_y, 8, LANES))
                moved = shifted(parts[1], parts[0], parts[2])
                for dz in range(3):
                    q[dz, b, dst_x, dst_y] = moved[dz].reshape(rows_x, rows_y, 8, LANES)
        for dy in range(3):
            for dz in range(3):
                k = dy * 3 + dz
                for x, end in ((1, 9),) if inner else ((0, 1), (9, 10)):
                    window = q[dz, b, x:end, dy : dy + 8].reshape((end - x) * PLANE, LANES)
                    lanes = slice(k * LANES, (k + 1) * LANES)
                    cols[b, x * PLANE : end * PLANE, lanes] = window.astype(BF16)


def tall(values, width):
    values = values.astype(F32)
    filler = jnp.zeros((LANES - width, values.shape[1]), F32)
    return jnp.concatenate([values, filler], axis=0).T


def fold_counts(width):
    each = width // (LANES - width)
    folded = TAPS // (each + 1)
    return folded * each, folded


def fold(terms, start, rows, width, matrix):
    main, folded = fold_counts(width)
    lane = lax.broadcasted_iota(jnp.int32, (width, LANES), 1)
    room = LANES - width
    each = width // room
    for j in range(main):
        chunk = j % each
        extra = pltpu.roll(matrix(main + j // each), (width - room * chunk) % LANES, 1)
        at = start + j * width
        terms[at : at + width, :] = jnp.where(lane < width, matrix(j), extra)
    for j in range(main + folded, TAPS):
        at = start + (j - folded) * width
        terms[at : at + width, :] = matrix(j)
    used = (TAPS - folded) * width
    terms[start + used : start + rows, :] = jnp.zeros((rows - used, LANES), F32)


class Stream:
    def __init__(self, number, start, rows, order, place, refs):
        self.number, self.base, self.length, self.order = number, start, rows, order
        self.at = start
        self.place = place
        self.terms, self.stage, self.landing, self.whole, self.send_sem, self.recv_sem = refs
        self.step = 0
        self.copies = []
        self.sent = []
        self.slot = 0

    def ds(self, start, size):
        return pl.ds(pl.multiple_of(start, 16), size)

    def send(self, src, dst, axis, other):
        copy = pltpu.make_async_remote_copy(
            src_ref=src,
            dst_ref=dst,
            send_sem=self.send_sem.at[self.number, self.slot],
            recv_sem=self.recv_sem.at[self.number, self.slot],
            device_id={axis: other},
            device_id_type=pl.DeviceIdType.MESH,
        )
        copy.start()
        self.slot += 1
        self.copies.append(copy)
        self.sent.append(copy)

    def start(self):
        count = len(self.order)
        self.copies = []
        if self.step < count:
            axis, low, radix = self.order[self.step]
            digit, others = peers(self.place, axis, low, radix)
            chunk = self.length // radix
            self.slots = []
            for theirs, other in others:
                here = slice(self.at, self.at + chunk)
                values = self.terms[self.ds(self.base + theirs * chunk, chunk), :]
                self.stage[here, :] = values.astype(BF16)
                rows = pl.ds(self.at, chunk)
                self.send(self.stage.at[rows], self.landing.at[rows], axis, other)
                self.slots.append(here)
                self.at += chunk
        else:
            axis, low, radix = self.order[2 * count - 1 - self.step]
            _, others = peers(self.place, axis, low, radix)
            here = self.whole.at[self.ds(self.base, self.length)]
            for _, other in others:
                self.send(here, here, axis, other)

    def finish(self):
        count = len(self.order)
        for copy in self.copies:
            copy.wait_recv()
        if self.step < count:
            axis, low, radix = self.order[self.step]
            digit, _ = peers(self.place, axis, low, radix)
            chunk = self.length // radix
            keep = self.base + digit * chunk
            value = self.terms[self.ds(keep, chunk), :]
            for here in self.slots:
                value = value + self.landing[here, :].astype(F32)
            if self.step == count - 1:
                self.whole[self.ds(keep, chunk), :] = value.astype(BF16)
            else:
                self.terms[self.ds(keep, chunk), :] = value
            self.base, self.length = keep, chunk
        else:
            axis, low, radix = self.order[2 * count - 1 - self.step]
            digit, _ = peers(self.place, axis, low, radix)
            self.base = self.base - digit * self.length
            self.length *= radix
        self.step += 1

    def done(self):
        return self.step == 2 * len(self.order)

    def advance(self):
        if not self.done():
            self.finish()
            if not self.done():
                self.start()

    def close(self):
        for copy in self.sent:
            copy.wait_send()


def peers(place, axis, low, radix):
    unit = 1 << low
    digit = (place[axis] // unit) % radix
    others = []
    for step in range(1, radix):
        theirs = (digit + step) % radix
        others.append((theirs, place[axis] + (theirs - digit) * unit))
    return digit, others


def step_kernel(
    blocks, width, sizes, orders, stream_rows,
    feat_far, cot_far, one_far, two_far, occ, near,
    out_far, total_far,
    out, out_sem, feat, cot, one, two, in_sem, part_z, part_g,
    local_a, local_g, low_a, high_a, low_g, high_g, q, cols_a, cols_g, weight_one, weight_two,
    spread_a, spread_g, send_first, send_last, land_low, land_high,
    hidden_first, hidden_last, hidden_low, hidden_high,
    terms, stage, landing, whole, send_sem, recv_sem, rim_send, rim_recv,
):
    taps = 9 * LANES
    span = 8 * PLANE
    rim_rows = blocks * PLANE
    place = {axis: lax.axis_index(axis) for axis in sizes}
    dev, count = place["dev"], sizes["dev"]
    has_low = dev > 0
    has_high = dev < count - 1
    low_dev = (dev + count - 1) % count
    high_dev = (dev + 1) % count

    loads = [
        pltpu.make_async_copy(src, dst, in_sem.at[i])
        for i, (src, dst) in enumerate(
            ((feat_far, feat), (cot_far, cot), (one_far, one), (two_far, two))
        )
    ]
    for load in loads:
        load.start()
    for ref in (land_low, land_high, hidden_low, hidden_high):
        ref[...] = jnp.zeros_like(ref)

    barrier = pltpu.get_barrier_semaphore()

    def greet(axis, other):
        pl.semaphore_signal(
            barrier, inc=1, device_id={axis: other}, device_id_type=pl.DeviceIdType.MESH
        )

    greeted = 0
    for phase in orders[0]:
        for _, other in peers(place, *phase)[1]:
            greet(phase[0], other)
            greeted += 1

    @pl.when(has_low)
    def _():
        greet("dev", low_dev)

    @pl.when(has_high)
    def _():
        greet("dev", high_dev)

    def rim_copy(which, src, dst, other):
        return pltpu.make_async_remote_copy(
            src_ref=src,
            dst_ref=dst,
            send_sem=rim_send.at[which],
            recv_sem=rim_recv.at[which],
            device_id={"dev": other},
            device_id_type=pl.DeviceIdType.MESH,
        )

    rim_copies = [
        rim_copy(0, send_last, land_low, high_dev),
        rim_copy(1, send_first, land_high, low_dev),
        rim_copy(2, hidden_last, hidden_low, high_dev),
        rim_copy(3, hidden_first, hidden_high, low_dev),
    ]

    def rims_go(first):
        @pl.when(has_high)
        def _():
            rim_copies[first].start()

        @pl.when(has_low)
        def _():
            rim_copies[first + 1].start()

    def rims_here(first):
        @pl.when(has_low)
        def _():
            rim_copies[first].wait_recv()

        @pl.when(has_high)
        def _():
            rim_copies[first + 1].wait_recv()

    def rims_gone(first):
        @pl.when(has_high)
        def _():
            rim_copies[first].wait_send()

        @pl.when(has_low)
        def _():
            rim_copies[first + 1].wait_send()

    mask_row = (occ[...] > 0).astype(F32)
    loads[0].wait()
    loads[1].wait()
    for kind, source, local in ((0, feat, local_a), (1, cot, local_g)):
        value = tall(source[...].astype(F32) * mask_row, width)
        local[0:blocks] = value.reshape(blocks, 8, 8, 8, LANES)
        local[blocks] = jnp.zeros((8, 8, 8, LANES), F32)
        for b in range(blocks):
            at = kind * rim_rows + b * PLANE
            send_first[at : at + PLANE, :] = value[b * span : b * span + PLANE].astype(BF16)
            send_last[at : at + PLANE, :] = value[(b + 1) * span - PLANE : (b + 1) * span].astype(BF16)

    pl.semaphore_wait(barrier, greeted + has_low.astype(jnp.int32) + has_high.astype(jnp.int32))
    rims_go(0)

    mask = jnp.broadcast_to(mask_row, (LANES, blocks * span)).T
    weight_one[...] = jnp.zeros_like(weight_one)
    weight_two[...] = jnp.zeros_like(weight_two)
    loads[2].wait()
    loads[3].wait()
    for t in range(TAPS):
        weight_one[t * LANES : t * LANES + width, 0:width] = one[t]
        weight_two[0:width, t * LANES : t * LANES + width] = two[TAPS - 1 - t]
    spread_a[...] = jnp.zeros_like(spread_a)
    spread_g[...] = jnp.zeros_like(spread_g)

    def widen(arrived, start, rim):
        value = arrived[start : start + rim_rows, :].astype(F32)
        rim[0:blocks] = value.reshape(blocks, 8, 8, LANES)
        rim[blocks] = jnp.zeros((8, 8, LANES), F32)

    def conv(cols, weight, b, steps):
        y = None
        for dx in steps:
            term = jnp.dot(
                cols[b, dx * PLANE : dx * PLANE + span, :],
                weight[dx * taps : (dx + 1) * taps, :],
                preferred_element_type=F32,
            )
            y = term if y is None else y + term
        return y

    def conv_back(b, steps):
        y = None
        for dx in steps:
            term = lax.dot_general(
                cols_g[b, dx * PLANE : dx * PLANE + span, :],
                weight_two[:, dx * taps : (dx + 1) * taps],
                (((1,), (1,)), ((), ())),
                preferred_element_type=F32,
            )
            y = term if y is None else y + term
        return y

    build_windows(blocks, local_a, low_a, high_a, near, q, cols_a, True)
    for b in range(blocks):
        part_z[b] = conv(cols_a, weight_one, b, (1,))
    build_windows(blocks, local_g, low_g, high_g, near, q, cols_g, True)
    for b in range(blocks):
        part_g[b] = conv_back(b, (1,))

    rims_here(0)
    for kind, low, high in ((0, low_a, high_a), (1, low_g, high_g)):
        widen(land_low, kind * rim_rows, low)
        widen(land_high, kind * rim_rows, high)

    refs = (terms, stage, landing, whole, send_sem, recv_sem)
    streams = [
        Stream(i, i * stream_rows, stream_rows, orders[i % 2], place, refs) for i in range(4)
    ]

    def outer(spread, cols):
        sums = None
        for b in range(blocks):
            part = lax.dot_general(
                spread[b], cols[b], (((0,), (0,)), ((), ())), preferred_element_type=F32
            )
            sums = part if sums is None else sums + part
        return sums

    build_windows(blocks, local_a, low_a, high_a, near, q, cols_a, False)
    zs = []
    for b in range(blocks):
        here = slice(b * span, (b + 1) * span)
        z = (part_z[b] + conv(cols_a, weight_one, b, (0, 2))) * mask[here]
        zs.append(z)
        hidden = (z * (1.0 / (1.0 + jnp.exp(-z)))).astype(BF16)
        hidden_first[b * PLANE : (b + 1) * PLANE, :] = hidden[0:PLANE]
        hidden_last[b * PLANE : (b + 1) * PLANE, :] = hidden[span - PLANE : span]
        local_a[b] = hidden.astype(F32).reshape(8, 8, 8, LANES)
        for dx in range(3):
            rows = slice(dx * PLANE, dx * PLANE + span)
            spread_a[b, rows, dx * LANES : (dx + 1) * LANES] = hidden
    rims_go(2)

    build_windows(blocks, local_g, low_g, high_g, near, q, cols_g, False)
    sums = outer(spread_a, cols_g)

    def second_matrix(j):
        dx, k = (TAPS - 1 - j) // 9, (TAPS - 1 - j) % 9
        return sums[dx * LANES : dx * LANES + width, k * LANES : (k + 1) * LANES]

    fold(terms, 0, 2 * stream_rows, width, second_matrix)
    for stream in streams[:2]:
        stream.start()

    for b in range(blocks):
        ga = part_g[b] + conv_back(b, (0, 2))
        z = zs[b]
        ga = ga * mask[b * span : (b + 1) * span]
        sigma = 1.0 / (1.0 + jnp.exp(-z))
        gz = (ga * sigma * (1.0 + z * (1.0 - sigma))).astype(BF16)
        for dx in range(3):
            rows = slice(dx * PLANE, dx * PLANE + span)
            spread_g[b, rows, dx * LANES : (dx + 1) * LANES] = gz
    for stream in streams[:2]:
        stream.advance()
    crossed = outer(spread_g, cols_a)

    def first_matrix(j):
        dx, k = j // 9, j % 9
        return crossed[dx * LANES : (dx + 1) * LANES, k * LANES : (k + 1) * LANES].T[0:width]

    fold(terms, 2 * stream_rows, 2 * stream_rows, width, first_matrix)
    for stream in streams[2:]:
        stream.start()
    for stream in streams[:2]:
        stream.advance()

    rims_here(2)
    widen(hidden_low, 0, low_a)
    widen(hidden_high, 0, high_a)
    for t in range(TAPS):
        weight_one[t * LANES : t * LANES + width, 0:width] = two[t]
    build_windows(blocks, local_a, low_a, high_a, near, q, cols_a, True)
    build_windows(blocks, local_a, low_a, high_a, near, q, cols_a, False)
    for stream in streams:
        stream.advance()
    for b in range(blocks):
        here = slice(b * span, (b + 1) * span)
        y = conv(cols_a, weight_one, b, (0, 1, 2))
        out[:, here] = (y.T[0:width] * mask_row[:, here]).astype(BF16)
        for stream in streams:
            stream.advance()
    stores = [pltpu.make_async_copy(out, out_far, out_sem.at[0])]
    stores[0].start()

    def store_half(which):
        rows = pl.ds(which * 2 * stream_rows, 2 * stream_rows)
        store = pltpu.make_async_copy(whole.at[rows], total_far.at[rows], out_sem.at[1 + which])
        store.start()
        stores.append(store)

    while not all(stream.done() for stream in streams[:2]):
        for stream in streams:
            stream.advance()
    store_half(0)
    while not all(stream.done() for stream in streams):
        for stream in streams:
            stream.advance()
    store_half(1)
    for stream in streams:
        stream.close()
    rims_gone(0)
    rims_gone(2)
    for store in stores:
        store.wait()


def unfold_kernel(
    width, scale, total_far, features, out, one_far, two_far, total, grad_one, grad_two, sem
):
    main, folded = fold_counts(width)
    each = main // folded
    half = total.shape[0] // 2
    loads = [
        pltpu.make_async_copy(
            total_far.at[pl.ds(i * half, half)], total.at[pl.ds(i * half, half)], sem.at[i]
        )
        for i in range(2)
    ]
    stores = []
    for copy in loads:
        copy.start()
    out[...] = features[...]
    for i, grad, far in ((0, grad_two, two_far), (1, grad_one, one_far)):
        start = i * half
        loads[i].wait()

        def rows(place):
            at = start + place * width
            return total[at : at + width, :].astype(F32) * scale

        for group in range(folded):
            spare = []
            for chunk in range(each):
                value = rows(group * each + chunk)
                grad[group * each + chunk] = value[:, 0:width]
                spare.append(value[:, width:LANES])
            grad[main + group] = jnp.concatenate(spare, axis=1)
        for j in range(main + folded, TAPS):
            grad[j] = rows(j - folded)[:, 0:width]
        store = pltpu.make_async_copy(grad, far, sem.at[2 + i])
        store.start()
        stores.append(store)
    for store in stores:
        store.wait()


def phases_of(axis, size, first):
    bits = size.bit_length() - 1
    phases = []
    while first < bits:
        step = min(2, bits - first)
        phases.append((axis, first, 1 << step))
        first += step
    return phases


def per_device(sizes, features_in, occupancy, cotangent, kernel_one, kernel_two, neighbours):
    width, voxels = features_in.shape
    blocks = neighbours.shape[0]
    devices = math.prod(sizes.values())
    scale = float(voxels * devices) ** (-0.5)
    vmem = pl.BlockSpec(memory_space=pltpu.VMEM)
    smem = pl.BlockSpec(memory_space=pltpu.SMEM)
    limit = 56 * 1024 * 1024

    core = [("group", 0, 2)]
    beside = [("dev", 0, 2)]
    across = phases_of("group", sizes["group"], 1)
    along = phases_of("dev", sizes["dev"], 1)
    orders = [core + beside + across + along, core + across + beside + along]
    slots = 2 * sum(radix - 1 for _, _, radix in orders[0])
    _, folded = fold_counts(width)
    used = (TAPS - folded) * width
    unit = 16 * devices
    stream_rows = -(-used // (2 * unit)) * unit
    rows = 4 * stream_rows

    rim = pltpu.VMEM((blocks + 1, 8, 8, LANES), F32)
    cube = pltpu.VMEM((blocks + 1, 8, 8, 8, LANES), F32)
    cols = pltpu.VMEM((blocks, 10 * PLANE, 9 * LANES), BF16)
    spread = pltpu.VMEM((blocks, 10 * PLANE, 3 * LANES), BF16)
    both_rims = pltpu.VMEM((2 * blocks * PLANE, LANES), BF16)
    one_rim = pltpu.VMEM((blocks * PLANE, LANES), BF16)
    packed = pltpu.VMEM((rows, LANES), BF16)
    features, total = pl.pallas_call(
        functools.partial(step_kernel, blocks, width, sizes, orders, stream_rows),
        out_shape=(
            jax.ShapeDtypeStruct((width, voxels), BF16),
            jax.ShapeDtypeStruct((rows, LANES), BF16),
        ),
        in_specs=[pl.BlockSpec(memory_space=pl.ANY)] * 4 + [vmem, smem],
        out_specs=[pl.BlockSpec(memory_space=pl.ANY)] * 2,
        scratch_shapes=[pltpu.VMEM((width, voxels), BF16), pltpu.SemaphoreType.DMA((3,))]
        + [pltpu.VMEM((width, voxels), BF16)] * 2
        + [pltpu.VMEM((TAPS, width, width), BF16)] * 2
        + [pltpu.SemaphoreType.DMA((4,))]
        + [pltpu.VMEM((blocks, 8 * PLANE, LANES), F32)] * 2
        + [cube, cube, rim, rim, rim, rim]
        + [pltpu.VMEM((3, blocks, 10, 10, 8, LANES), F32), cols, cols]
        + [pltpu.VMEM((TAPS * LANES, LANES), BF16), pltpu.VMEM((LANES, TAPS * LANES), BF16)]
        + [spread, spread]
        + [both_rims] * 4
        + [one_rim] * 4
        + [pltpu.VMEM((rows, LANES), F32), packed, packed, packed]
        + [pltpu.SemaphoreType.DMA((4, slots))] * 2
        + [pltpu.SemaphoreType.DMA((4,))] * 2,
        compiler_params=pltpu.CompilerParams(
            collective_id=0, has_side_effects=True, vmem_limit_bytes=limit
        ),
        name="train_step",
    )(features_in, cotangent, kernel_one, kernel_two, occupancy[None, :], neighbours)
    return pl.pallas_call(
        functools.partial(unfold_kernel, width, scale),
        out_shape=(
            jax.ShapeDtypeStruct((width, voxels), BF16),
            jax.ShapeDtypeStruct((TAPS, width, width), F32),
            jax.ShapeDtypeStruct((TAPS, width, width), F32),
        ),
        in_specs=[pl.BlockSpec(memory_space=pl.ANY), vmem],
        out_specs=[vmem] + [pl.BlockSpec(memory_space=pl.ANY)] * 2,
        scratch_shapes=[pltpu.VMEM((rows, LANES), BF16)]
        + [pltpu.VMEM((TAPS, width, width), F32)] * 2
        + [pltpu.SemaphoreType.DMA((4,))],
        compiler_params=pltpu.CompilerParams(vmem_limit_bytes=limit),
        name="unfold",
    )(total, features)


def solution(mesh):
    sizes = dict(mesh.shape)
    return jax.shard_map(
        functools.partial(per_device, sizes),
        mesh=mesh,
        in_specs=(
            P(None, ("group", "dev")),
            P(("group", "dev")),
            P(None, ("group", "dev")),
            P(),
            P(),
            P(("group", "dev"), None),
        ),
        out_specs=(P(None, ("group", "dev")), P(), P()),
        check_vma=False,
    )
```
